32 devices in a mesh: noise: 2 (over x), row: 4 (over y, core), col: 4 (over z).
Axes of the slice: x: 2, y: 2, z: 4, core: 2. Of those that a mesh axis runs over, the one named last changes fastest.
Arguments:
- image: bfloat16 [256, 128, 128], P(('noise', 'row'), 'col'), parts along dimension 0, may hold values from -6 to 6
- noise_level: int32 [2], P('noise'), parts along dimension 0, may hold values from 0 to 7
- cond_table: float32 [8, 256], replicated, may hold values from -6 to 6
- ada_fine: float32 [256, 128], replicated, may hold values from -0.375 to 0.375
- fine_qkv: bfloat16 [128, 384], replicated, may hold values from -0.5 to 0.5
- fine_scale: float32 [2], replicated, may hold values from 4 to 16
- fine_out_w: bfloat16 [128, 128], replicated, may hold values from -0.5 to 0.5
- fine_post: float32 [128], replicated, may hold values from 0.1 to 1.9
- merge_w: bfloat16 [512, 256], replicated, may hold values from -0.25 to 0.25
- coarse_in_w: bfloat16 [256, 1024], replicated, may hold values from -0.375 to 0.375
- ada_coarse: float32 [256, 1024], replicated, may hold values from -0.375 to 0.375
- coarse_qkv: bfloat16 [3, 1024, 1024], P(None, None, 'col'), may hold values from -0.1875 to 0.1875
- coarse_scale: float32 [16], P('col'), may hold values from 4 to 16
- coarse_out_w: bfloat16 [1024, 1024], P('col'), may hold values from -0.1875 to 0.1875
- coarse_post: float32 [1024], replicated, may hold values from 0.1 to 1.9
Outputs:
- fine_out: bfloat16 [256, 128, 128], P(('noise', 'row'), 'col'), parts along dimension 0
- coarse_out: bfloat16 [16, 8, 1024], P(('noise', 'row'), 'col'), parts along dimension 0
The draws below stay inside these ranges and needn't reach their ends.
There are 2 independent parts, one for each index of `noise`. The reference program is written for one: setup_inputs(seed, part) draws one part's arguments, and reference() takes and returns one part's arrays. A program takes and returns all parts, laid end to end along the dimension named above; an argument that names none is the same for every part. Nothing has to cross between parts.
All inputs are finite; a program needn't handle non-finite values.
Results may differ from the reference program's by a relative error of at most 0.035.
Values may be sent and summed in bfloat16 or wider, within the bound.
A program may use at most 128 MiB of HBM per device.

```python
import math
import jax
import jax.numpy as jnp
from jax import lax

D = 128
HEAD = 64
HF = 2
DM = 256
DC = 1024
HC = 16
COND = 256
NLEV = 8
TILE = 32
POOL = 8
NR = 128
NC = 128
PR = 8
PC = 8


def block_scale(stream_key, dims, split, low, high):
    gain, own = 1.0, jax.random.fold_in(stream_key, 6)
    for axis_at, parts in split:
        steps = jnp.exp(jax.random.uniform(jax.random.fold_in(own, axis_at), (parts,), jnp.float32, low / len(split), high / len(split)))
        gain = gain * jnp.repeat(steps, dims[axis_at] // parts).reshape([-1 if axis == axis_at else 1 for axis in range(len(dims))])
    return gain


def centred(own_key, extent, spread, most, shards=(), held_as=jnp.bfloat16):
    values = spread * jax.random.normal(own_key, extent, jnp.float32)
    if shards:
        values = values * block_scale(own_key, extent, shards, -0.22, 0.18)
    return jnp.clip(values, -most, most).astype(held_as)


def setup_inputs(seed: int = 0, part: int = 0) -> dict:
    splits = jax.random.split(jax.random.key(seed), 16)
    part_keys = jax.random.split(jax.random.fold_in(splits[15], part), 16)
    image = centred(part_keys[0], (NR, NC, D), 1.0, 6.0, ((0, 4), (1, 4)))
    noise_level = jax.random.randint(part_keys[1], (1,), 0, NLEV).astype(jnp.int32)
    cond_table = centred(splits[2], (NLEV, COND), 1.0, 6.0, (), jnp.float32)
    ada_fine = centred(splits[3], (COND, D), COND ** -0.5, 0.375, (), jnp.float32)
    fine_qkv = centred(splits[4], (D, 3 * D), D ** -0.5, 0.5)
    fine_scale = jnp.clip(jnp.exp(jax.random.uniform(splits[5], (HF,), jnp.float32, math.log(4.0), math.log(16.0))), 4.0, 16.0)
    fine_out_w = centred(splits[6], (D, D), D ** -0.5, 0.5)
    fine_post = jnp.clip(1.0 + 0.18 * jax.random.normal(splits[7], (D,), jnp.float32), 0.1, 1.9)
    merge_w = centred(splits[8], (4 * D, DM), (4 * D) ** -0.5, 0.25)
    coarse_in_w = centred(splits[9], (DM, DC), DM ** -0.5, 0.375)
    ada_coarse = centred(splits[10], (COND, DC), COND ** -0.5, 0.375, (), jnp.float32)
    coarse_qkv = centred(splits[11], (3, DC, DC), DC ** -0.5, 0.1875, ((2, 4),))
    coarse_scale = jnp.clip(jnp.exp(math.log(16.0) - 1.3862944 * jax.random.uniform(splits[12], (HC,), jnp.float32) ** block_scale(splits[12], (HC,), ((0, 4),), -0.2, 0.2)), 4.0, 16.0)
    coarse_out_w = centred(splits[13], (DC, DC), DC ** -0.5, 0.1875, ((0, 4),))
    coarse_post = jnp.clip(1.0 + 0.18 * jax.random.normal(splits[14], (DC,), jnp.float32), 0.1, 1.9)
    return {"image": image, "noise_level": noise_level, "cond_table": cond_table, "ada_fine": ada_fine, "fine_qkv": fine_qkv, "fine_scale": fine_scale, "fine_out_w": fine_out_w, "fine_post": fine_post, "merge_w": merge_w, "coarse_in_w": coarse_in_w, "ada_coarse": ada_coarse, "coarse_qkv": coarse_qkv, "coarse_scale": coarse_scale, "coarse_out_w": coarse_out_w, "coarse_post": coarse_post}


def rms(value):
    return value * lax.rsqrt(lax.optimization_barrier(jnp.mean(value * value, axis=-1, keepdims=True)) + 1e-06)

def cosine(value, heads):
    shaped = value.reshape(value.shape[:-1] + (heads, HEAD))
    return rms(shaped).reshape(value.shape)

def attend(queries, keys, values, valid, scale, heads):
    results = []
    for head in range(heads):
        low = head * HEAD
        scores = jnp.dot(queries[:, low:low + HEAD], keys[:, low:low + HEAD].T, preferred_element_type=jnp.float32)
        scores = scores * (scale[head] / HEAD)
        if valid is not None:
            scores = jnp.where(valid[None, :], scores, -jnp.inf)
        top = lax.optimization_barrier(jnp.max(scores, axis=-1, keepdims=True))
        expo = jnp.exp(scores - top)
        if valid is not None:
            expo = jnp.where(valid[None, :], expo, 0.0)
        weights = (expo / lax.optimization_barrier(jnp.sum(expo, axis=-1, keepdims=True))).astype(jnp.bfloat16)
        results.append(jnp.dot(weights, values[:, low:low + HEAD], preferred_element_type=jnp.float32))
    return jnp.concatenate(results, axis=-1).astype(jnp.bfloat16)

def reference(image, noise_level, cond_table, ada_fine, fine_qkv, fine_scale, fine_out_w, fine_post, merge_w, coarse_in_w, ada_coarse, coarse_qkv, coarse_scale, coarse_out_w, coarse_post):
    highest = lax.Precision.HIGHEST
    levels = jnp.arange(NLEV, dtype=jnp.int32)
    hot = (levels == noise_level[0]).astype(jnp.float32)
    cond = jnp.dot(hot, cond_table, precision=highest)
    fine_gain = 1.0 + jnp.dot(cond, ada_fine, precision=highest)
    coarse_gain = 1.0 + jnp.dot(cond, ada_coarse, precision=highest)
    xfull = image.astype(jnp.float32)
    xn = (rms(xfull) * fine_gain).astype(jnp.bfloat16)
    qkv = jnp.dot(xn.reshape(-1, D), fine_qkv, preferred_element_type=jnp.float32).reshape(NR, NC, 3 * D)
    queries = cosine(qkv[..., :D], HF).astype(jnp.bfloat16)
    keys = cosine(qkv[..., D:2 * D], HF).astype(jnp.bfloat16)
    values = qkv[..., 2 * D:].astype(jnp.bfloat16)
    keys_pad = jnp.pad(keys, ((TILE, TILE), (TILE, TILE), (0, 0)))
    values_pad = jnp.pad(values, ((TILE, TILE), (TILE, TILE), (0, 0)))
    row_ids = jnp.arange(NR + 2 * TILE, dtype=jnp.int32) - TILE
    col_ids = jnp.arange(NC + 2 * TILE, dtype=jnp.int32) - TILE
    inside = ((row_ids >= 0) & (row_ids < NR))[:, None] & ((col_ids >= 0) & (col_ids < NC))[None, :]
    tile_cols = NC // TILE
    tile_rows = NR // TILE

    def one_tile(index):
        trow = (index // tile_cols).astype(jnp.int32)
        tcol = (index % tile_cols).astype(jnp.int32)
        zero = jnp.zeros((), jnp.int32)
        q_tile = lax.dynamic_slice(queries, (trow * TILE, tcol * TILE, zero), (TILE, TILE, D)).reshape(TILE * TILE, D)
        k_win = lax.dynamic_slice(keys_pad, (trow * TILE, tcol * TILE, zero), (3 * TILE, 3 * TILE, D)).reshape(-1, D)
        v_win = lax.dynamic_slice(values_pad, (trow * TILE, tcol * TILE, zero), (3 * TILE, 3 * TILE, D)).reshape(-1, D)
        valid = lax.dynamic_slice(inside, (trow * TILE, tcol * TILE), (3 * TILE, 3 * TILE)).reshape(-1)
        return attend(q_tile, k_win, v_win, valid, fine_scale, HF)
    tiles = lax.map(one_tile, jnp.arange(tile_rows * tile_cols, dtype=jnp.int32))
    attended = tiles.reshape(tile_rows, tile_cols, TILE, TILE, D).transpose(0, 2, 1, 3, 4).reshape(NR, NC, D)
    branch = jnp.dot(attended.reshape(-1, D), fine_out_w, preferred_element_type=jnp.float32).reshape(NR, NC, D)
    fine_out = (xfull + rms(branch) * fine_post).astype(jnp.bfloat16)
    blocks = fine_out.reshape(NR // 2, 2, NC // 2, 2, D).transpose(0, 2, 1, 3, 4).reshape(-1, 4 * D)
    merged = jnp.dot(blocks, merge_w, preferred_element_type=jnp.float32).astype(jnp.bfloat16)
    merged = merged.reshape(PR, POOL, PC, POOL, DM).astype(jnp.float32)
    pooled = lax.optimization_barrier(jnp.mean(merged, axis=(1, 3))).astype(jnp.bfloat16).reshape(-1, DM)
    coarse_in = jnp.dot(pooled, coarse_in_w, preferred_element_type=jnp.float32)
    cn = (rms(coarse_in) * coarse_gain).astype(jnp.bfloat16)
    qc = cosine(jnp.dot(cn, coarse_qkv[0], preferred_element_type=jnp.float32), HC).astype(jnp.bfloat16)
    kc = cosine(jnp.dot(cn, coarse_qkv[1], preferred_element_type=jnp.float32), HC).astype(jnp.bfloat16)
    vc = jnp.dot(cn, coarse_qkv[2], preferred_element_type=jnp.float32).astype(jnp.bfloat16)
    coarse_attended = attend(qc, kc, vc, None, coarse_scale, HC)
    coarse_branch = jnp.dot(coarse_attended, coarse_out_w, preferred_element_type=jnp.float32)
    coarse_out = (coarse_in + rms(coarse_branch) * coarse_post).astype(jnp.bfloat16).reshape(PR, PC, DC)
    return (fine_out, coarse_out)
```

```python
import functools
import math

import jax
import jax.numpy as jnp
from jax import lax
from jax.experimental import pallas as pl
from jax.experimental.pallas import tpu as pltpu
from jax.sharding import PartitionSpec as P

HEAD = 64
TILE = 32
POOL = 8
QB = 256
EPS = 1e-6
MESH = pl.DeviceIdType.MESH
HIGHEST = lax.Precision.HIGHEST
BF = jnp.bfloat16
F32 = jnp.float32
SWAP = (0, 2, 1)


def mm(a, b):
    return jnp.dot(a, b, preferred_element_type=F32)


def iota(shape, dim):
    return lax.broadcasted_iota(jnp.int32, shape, dim)


def kernel(
    nrow, ncol, level_ref, fscale_ref, cscale_ref, image_ref, table_ref, ada_fine_ref, fqkv_ref,
    fout_ref, fpost_ref, cpost_ref, merge_hbm, cin_hbm, adac_hbm, cqkv_hbm, cout_hbm,
    fine_ref, coarse_ref,
    slots, qs, kt, vext, acc, merge_w, cin_w, adac_w, cqkv_w, cout_w, gath, pack, qall,
    sbuf, rbuf, local_sem, hsend, hrecv, gsend, grecv, rsend, rrecv,
):
    tokens, width = image_ref.shape
    ndev = nrow * ncol
    row, col = lax.axis_index("row"), lax.axis_index("col")
    me = row * ncol + col
    sib = 1 - 2 * lax.rem(row, 2)

    barrier = pltpu.get_barrier_semaphore()

    def greet(i, carry):
        peer = lax.rem(me + i, ndev)
        pl.semaphore_signal(
            barrier, inc=1, device_id={"row": peer // ncol, "col": lax.rem(peer, ncol)},
            device_id_type=MESH,
        )
        return carry

    lax.fori_loop(1, ndev, greet, 0)
    loads = [
        pltpu.make_async_copy(src, dst, local_sem.at[i])
        for i, (src, dst) in enumerate(
            ((merge_hbm, merge_w), (cin_hbm, cin_w), (adac_hbm, adac_w), (cqkv_hbm, cqkv_w),
             (cout_hbm, cout_w))
        )
    ]
    for load in loads:
        load.start()

    levels = table_ref.shape[0]
    hot = iota((levels, 1), 0) == level_ref[0]
    cond = jnp.sum(jnp.where(hot, table_ref[...], 0.0), axis=0, keepdims=True)
    cond = jnp.broadcast_to(cond, (8, cond.shape[1]))
    fine_gain = 1.0 + jnp.dot(cond, ada_fine_ref[...], precision=HIGHEST)[0:1]
    low = iota((1, width), 1) < HEAD
    same = (iota((width, width), 0) // HEAD) == (iota((width, width), 1) // HEAD)
    block_ones = jnp.where(same, 1.0, 0.0).astype(BF)

    def normed(x):
        x = x.astype(F32)
        return (x * lax.rsqrt(jnp.mean(x * x, axis=-1, keepdims=True) + EPS) * fine_gain).astype(BF)

    def cosine(x):
        total = mm((x * x).astype(BF), block_ones)
        return x * lax.rsqrt(total * (1.0 / HEAD) + EPS)

    factor = math.log2(math.e) / HEAD
    qscale = jnp.where(low, fscale_ref[0] * factor, fscale_ref[1] * factor)
    queries = cosine(mm(normed(image_ref[...]), fqkv_ref[:, 0:width])) * qscale
    qs[0] = jnp.where(low, queries, 0.0).astype(BF)
    qs[1] = jnp.where(low, 0.0, queries).astype(BF)
    slots[0] = image_ref[...]
    acc[...] = jnp.zeros_like(acc)

    pl.semaphore_wait(barrier, ndev - 1)

    def place(rc, bc):
        a = jnp.where(rc == 0, 0, jnp.where(rc == 1, sib, -sib))
        b = jnp.where(bc == 0, 0, jnp.where(bc == 1, -1, 1))
        r, c = row + a, col + b
        ok = (r >= 0) & (r < nrow) & (c >= 0) & (c < ncol)
        return r, c, ok

    def halo(rc, bc):
        r, c, ok = place(rc, bc)
        there = SWAP[bc] * 3 + rc
        copy = pltpu.make_async_remote_copy(
            src_ref=image_ref, dst_ref=slots.at[there], send_sem=hsend.at[bc * 3 + rc],
            recv_sem=hrecv.at[there], device_id={"row": r, "col": c}, device_id_type=MESH,
        )
        return copy, ok

    order = [(1, 0), (2, 0), (0, 1), (0, 2), (1, 1), (1, 2), (2, 1), (2, 2)]
    for rc, bc in order:
        copy, ok = halo(rc, bc)

        @pl.when(ok)
        def _():
            copy.start()

    def step(s, carry):
        _, _, ok = place(lax.rem(s, 3), s // 3)

        @pl.when(ok)
        def _():
            @pl.when(s > 0)
            def _():
                pltpu.make_async_remote_copy(
                    src_ref=image_ref, dst_ref=slots.at[s], send_sem=hsend.at[s],
                    recv_sem=hrecv.at[s], device_id={"row": row, "col": col}, device_id_type=MESH,
                ).wait_recv()

            proj = mm(normed(slots[s]), fqkv_ref[:, width:])
            keys = cosine(proj[:, 0:width])
            kt[...] = keys.T.astype(BF)
            values = proj[:, width:]
            vext[0] = jnp.where(low, values, 1.0).astype(BF)
            vext[1] = jnp.where(low, 1.0, values).astype(BF)

            def block(i, c2):
                rows = pl.ds(pl.multiple_of(i * QB, QB), QB)
                s0 = mm(qs[0, rows, :], kt[...])
                s1 = mm(qs[1, rows, :], kt[...])
                p0 = jnp.exp2(s0).astype(BF)
                acc[0, rows, :] += mm(p0, vext[0])
                p1 = jnp.exp2(s1).astype(BF)
                acc[1, rows, :] += mm(p1, vext[1])
                return c2

            lax.fori_loop(0, tokens // QB, block, 0)

        return carry

    lax.fori_loop(0, 9, step, 0)

    for load in loads:
        load.wait()
    coarse_gain = 1.0 + jnp.dot(cond, adac_w[...], precision=HIGHEST)[0:1]

    a0, a1 = acc[0], acc[1]
    num = jnp.where(low, a0, a1)
    den = pltpu.roll(jnp.where(low, a1, a0), HEAD, 1)
    attended = (num / den).astype(BF)
    branch = mm(attended, fout_ref[...])
    branch = branch * lax.rsqrt(jnp.mean(branch * branch, axis=-1, keepdims=True) + EPS)
    fine = (image_ref[...].astype(F32) + branch * fpost_ref[...]).astype(BF)
    fine_ref[...] = fine
    at = iota((64, tokens), 1)
    r, c = at // TILE, at % TILE
    span = 2 * POOL
    target = ((r % 2) * 2 + c % 2) * 16 + (r // span) * (TILE // span) + c // span
    pick = jnp.where(iota((64, tokens), 0) == target, 1.0, 0.0).astype(BF)
    sums = mm(pick, fine) * (1.0 / (POOL * POOL))
    high = sums.astype(BF)
    rest = (sums - high.astype(F32)).astype(BF)
    pooled = jnp.zeros((16, merge_w.shape[1]), F32)
    for p in range(4):
        part_w = merge_w[p * width : (p + 1) * width, :]
        pooled = pooled + mm(high[p * 16 : p * 16 + 16], part_w) + mm(rest[p * 16 : p * 16 + 16], part_w)
    coarse_in = mm(pooled.astype(BF), cin_w[...])
    cn = coarse_in * lax.rsqrt(jnp.mean(coarse_in * coarse_in, axis=-1, keepdims=True) + EPS) * coarse_gain
    quarter = coarse_in.shape[1] // 4
    for j in range(4):
        pack[4 * j : 4 * j + 4, :] = cn[0:4, j * quarter : (j + 1) * quarter]
    gath[me] = pack[...].astype(BF)

    def gather(i):
        peer = lax.rem(me + i, ndev)
        return pltpu.make_async_remote_copy(
            src_ref=gath.at[me], dst_ref=gath.at[me], send_sem=gsend.at[i], recv_sem=grecv.at[me],
            device_id={"row": peer // ncol, "col": lax.rem(peer, ncol)}, device_id_type=MESH,
        )

    def gather_from(i):
        peer = lax.rem(me + i, ndev)
        return pltpu.make_async_remote_copy(
            src_ref=gath.at[peer], dst_ref=gath.at[peer], send_sem=gsend.at[i],
            recv_sem=grecv.at[peer],
            device_id={"row": peer // ncol, "col": lax.rem(peer, ncol)}, device_id_type=MESH,
        )

    def loop(low_at, high_at, do):
        def one(i, carry):
            do(i)
            return carry

        lax.fori_loop(low_at, high_at, one, 0)

    loop(1, ndev, lambda i: gather(i).start())
    loop(1, ndev, lambda i: gather_from(i).wait_recv())

    every = gath[...].reshape(ndev * 16, quarter)
    lw = cqkv_w.shape[2]
    count = ndev * 4
    out_at, in_at = iota((count, ndev * 16), 0), iota((count, ndev * 16), 1)
    proj = [jnp.zeros((count, lw), F32) for _ in range(3)]
    for j in range(4):
        wanted = (out_at // 4) * 16 + j * 4 + out_at % 4
        chosen = mm(jnp.where(in_at == wanted, 1.0, 0.0).astype(BF), every).astype(BF)
        for k in range(3):
            proj[k] = proj[k] + mm(chosen, cqkv_w[k, j * quarter : (j + 1) * quarter, :])
    head_same = (iota((lw, lw), 0) // HEAD) == (iota((lw, lw), 1) // HEAD)
    head_ones = jnp.where(head_same, 1.0, 0.0)

    def ccosine(x):
        total = jnp.dot(x * x, head_ones, precision=HIGHEST)
        return x * lax.rsqrt(total * (1.0 / HEAD) + EPS)

    qall[...] = ccosine(proj[0])
    keys = ccosine(proj[1]).astype(BF)
    values = proj[2].astype(BF)
    own = ncol * 4
    queries = qall[pl.ds(pl.multiple_of(row * own, own), own), :]
    heads = lw // HEAD
    lane_head = iota((own, lw), 1) // HEAD
    stack = jnp.concatenate(
        [jnp.where(lane_head == h, queries, 0.0) for h in range(heads)], axis=0
    ).astype(BF)
    scores = lax.dot_general(stack, keys, (((1,), (1,)), ((), ())), preferred_element_type=F32)
    results = jnp.zeros((own, lw), F32)
    for h in range(heads):
        expo = jnp.exp(scores[h * own : (h + 1) * own] * (cscale_ref[h] / HEAD))
        weights = (expo / jnp.sum(expo, axis=-1, keepdims=True)).astype(BF)
        results = results + jnp.where(lane_head == h, mm(weights, values), 0.0)
    partial = mm(results.astype(BF), cout_w[...])
    for k in range(ncol):
        for j in range(4):
            pack[4 * j : 4 * j + 4, :] = partial[4 * k : 4 * k + 4, j * quarter : (j + 1) * quarter]
        sbuf[k] = pack[...].astype(BF)
    rbuf[col] = sbuf[col]

    def reduce(i):
        peer = lax.rem(col + i, ncol)
        return pltpu.make_async_remote_copy(
            src_ref=sbuf.at[peer], dst_ref=rbuf.at[col], send_sem=rsend.at[i],
            recv_sem=rrecv.at[col], device_id={"row": row, "col": peer}, device_id_type=MESH,
        )

    def reduce_from(i):
        peer = lax.rem(col + i, ncol)
        return pltpu.make_async_remote_copy(
            src_ref=sbuf.at[peer], dst_ref=rbuf.at[peer], send_sem=rsend.at[i],
            recv_sem=rrecv.at[peer], device_id={"row": row, "col": peer}, device_id_type=MESH,
        )

    loop(1, ncol, lambda i: reduce(i).start())
    loop(1, ncol, lambda i: reduce_from(i).wait_recv())
    total = jnp.sum(rbuf[...].astype(F32), axis=0)
    pack[...] = total
    pieces = [pack[4 * j : 4 * j + 4, :] for j in range(4)]
    power = sum(jnp.sum(piece * piece, axis=-1, keepdims=True) for piece in pieces)
    inverse = lax.rsqrt(power * (1.0 / (4 * quarter)) + EPS)
    for j in range(4):
        at_j = slice(j * quarter, (j + 1) * quarter)
        y = coarse_in[0:4, at_j] + pieces[j] * inverse * cpost_ref[:, at_j]
        coarse_ref[:, at_j] = y

    for rc, bc in order:
        copy, ok = halo(rc, bc)

        @pl.when(ok)
        def _():
            copy.wait_send()

    loop(1, ndev, lambda i: gather(i).wait_send())
    loop(1, ncol, lambda i: reduce(i).wait_send())


def body(
    image, noise_level, cond_table, ada_fine, fine_qkv, fine_scale, fine_out_w, fine_post,
    merge_w, coarse_in_w, ada_coarse, coarse_qkv, coarse_scale, coarse_out_w, coarse_post,
):
    nrow, ncol = lax.axis_size("row"), lax.axis_size("col")
    ndev = nrow * ncol
    rows, cols, width = image.shape
    tokens = rows * cols
    lw = coarse_qkv.shape[2]
    cw = coarse_in_w.shape[1]
    quarter = cw // 4
    smem = pl.BlockSpec(memory_space=pltpu.SMEM)
    vmem = pl.BlockSpec(memory_space=pltpu.VMEM)
    hbm = pl.BlockSpec(memory_space=pl.ANY)
    dma = pltpu.SemaphoreType.DMA
    fine, coarse = pl.pallas_call(
        functools.partial(kernel, nrow, ncol),
        out_shape=(
            jax.ShapeDtypeStruct((tokens, width), BF),
            jax.ShapeDtypeStruct((4, cw), F32),
        ),
        in_specs=[smem] * 3 + [vmem] * 7 + [hbm] * 5,
        out_specs=(vmem, vmem),
        scratch_shapes=[
            pltpu.VMEM((9, tokens, width), BF),
            pltpu.VMEM((2, tokens, width), BF),
            pltpu.VMEM((width, tokens), BF),
            pltpu.VMEM((2, tokens, width), BF),
            pltpu.VMEM((2, tokens, width), F32),
            pltpu.VMEM(merge_w.shape, BF),
            pltpu.VMEM(coarse_in_w.shape, BF),
            pltpu.VMEM(ada_coarse.shape, F32),
            pltpu.VMEM(coarse_qkv.shape, BF),
            pltpu.VMEM(coarse_out_w.shape, BF),
            pltpu.VMEM((ndev, 16, quarter), BF),
            pltpu.VMEM((16, quarter), F32),
            pltpu.VMEM((ndev * 4, lw), F32),
            pltpu.VMEM((ncol, 16, quarter), BF),
            pltpu.VMEM((ncol, 16, quarter), BF),
            dma((5,)), dma((9,)), dma((9,)), dma((ndev,)), dma((ndev,)), dma((ncol,)), dma((ncol,)),
        ],
        compiler_params=pltpu.CompilerParams(
            collective_id=0, has_side_effects=True, vmem_limit_bytes=48 * 1024 * 1024
        ),
        cost_estimate=pl.CostEstimate(
            flops=tokens * tokens * 9 * width * 4, bytes_accessed=8 << 20,
            transcendentals=tokens * tokens * 18,
        ),
    )(
        noise_level, fine_scale, coarse_scale, image.reshape(tokens, width), cond_table, ada_fine,
        fine_qkv, fine_out_w, fine_post.reshape(1, -1), coarse_post.reshape(1, -1), merge_w,
        coarse_in_w, ada_coarse, coarse_qkv, coarse_out_w,
    )
    side = TILE // (2 * POOL)
    return fine.reshape(rows, cols, width), coarse.astype(BF).reshape(side, side, cw)


def solution(mesh):
    in_specs = (
        P(("noise", "row"), "col", None),
        P("noise"),
        P(),
        P(),
        P(),
        P(),
        P(),
        P(),
        P(),
        P(),
        P(),
        P(None, None, "col"),
        P("col"),
        P("col", None),
        P(),
    )
    out_specs = (P(("noise", "row"), "col", None), P(("noise", "row"), "col", None))
    return jax.shard_map(body, mesh=mesh, in_specs=in_specs, out_specs=out_specs, check_vma=False)
```

```python
import functools
import math

import jax
import jax.numpy as jnp
from jax import lax
from jax.experimental import pallas as pl
from jax.experimental.pallas import tpu as pltpu
from jax.sharding import PartitionSpec as P

HEAD = 64
TILE = 32
POOL = 8
QB = 256
VMEM_BYTES = 64 * 1024 * 1024 - 65536
EPS = 1e-6
MESH = pl.DeviceIdType.MESH
HIGHEST = lax.Precision.HIGHEST
BF = jnp.bfloat16
F32 = jnp.float32
SWAP = (0, 2, 1)


def mm(a, b):
    return jnp.dot(a, b, preferred_element_type=F32)


def iota(shape, dim):
    return lax.broadcasted_iota(jnp.int32, shape, dim)


def kernel(
    nrow, ncol, level_ref, fscale_ref, cscale_ref, image_hbm, table_hbm, adaf_hbm, fqkv_hbm,
    fout_hbm, fpost_hbm, cpost_hbm, merge_hbm, cin_hbm, adac_hbm, cqkv_hbm, cout_hbm,
    fine_hbm, coarse_ref,
    slots, qs, kt, vext, acc, table_ref, ada_fine_ref, fqkv_ref, fout_ref, fpost_ref, cpost_ref,
    merge_w, cin_w, adac_w, cqkv_w, cout_w, fine_ref, gath, pack, qall,
    sbuf, rbuf, local_sem, hsend, hrecv, gsend, grecv, rsend, rrecv,
):
    tokens, width = image_hbm.shape
    image_ref = slots.at[0]
    ndev = nrow * ncol
    row, col = lax.axis_index("row"), lax.axis_index("col")
    me = row * ncol + col
    sib = 1 - 2 * lax.rem(row, 2)

    loads = [
        pltpu.make_async_copy(src, dst, local_sem.at[i])
        for i, (src, dst) in enumerate(
            ((image_hbm, image_ref), (table_hbm, table_ref), (adaf_hbm, ada_fine_ref),
             (fqkv_hbm, fqkv_ref), (adac_hbm, adac_w), (fout_hbm, fout_ref),
             (fpost_hbm, fpost_ref), (cpost_hbm, cpost_ref), (merge_hbm, merge_w),
             (cin_hbm, cin_w), (cqkv_hbm, cqkv_w), (cout_hbm, cout_w))
        )
    ]
    for load in loads:
        load.start()

    barrier = pltpu.get_barrier_semaphore()

    def greet(i, carry):
        peer = lax.rem(me + i, ndev)
        pl.semaphore_signal(
            barrier, inc=1, device_id={"row": peer // ncol, "col": lax.rem(peer, ncol)},
            device_id_type=MESH,
        )
        return carry

    lax.fori_loop(1, ndev, greet, 0)
    for load in loads[:4]:
        load.wait()
    levels = table_ref.shape[0]
    hot = iota((levels, 1), 0) == level_ref[0]
    cond = jnp.sum(jnp.where(hot, table_ref[...], 0.0), axis=0, keepdims=True)
    cond = jnp.broadcast_to(cond, (8, cond.shape[1]))
    fine_gain = 1.0 + jnp.dot(cond, ada_fine_ref[...], precision=HIGHEST)[0:1]
    low = iota((1, width), 1) < HEAD
    same = (iota((width, width), 0) // HEAD) == (iota((width, width), 1) // HEAD)
    block_ones = jnp.where(same, 1.0, 0.0).astype(BF)

    def normed(x):
        x = x.astype(F32)
        return (x * lax.rsqrt(jnp.mean(x * x, axis=-1, keepdims=True) + EPS) * fine_gain).astype(BF)

    def cosine(x):
        total = mm((x * x).astype(BF), block_ones)
        return x * lax.rsqrt(total * (1.0 / HEAD) + EPS)

    factor = math.log2(math.e) / HEAD
    qscale = jnp.where(low, fscale_ref[0] * factor, fscale_ref[1] * factor)
    queries = cosine(mm(normed(slots[0]), fqkv_ref[:, 0:width])) * qscale
    qs[0] = jnp.where(low, queries, 0.0).astype(BF)
    qs[1] = jnp.where(low, 0.0, queries).astype(BF)
    acc[...] = jnp.zeros_like(acc)
    loads[4].wait()
    coarse_gain = 1.0 + jnp.dot(cond, adac_w[...], precision=HIGHEST)[0:1]

    pl.semaphore_wait(barrier, ndev - 1)

    def place(rc, bc):
        a = jnp.where(rc == 0, 0, jnp.where(rc == 1, sib, -sib))
        b = jnp.where(bc == 0, 0, jnp.where(bc == 1, -1, 1))
        r, c = row + a, col + b
        ok = (r >= 0) & (r < nrow) & (c >= 0) & (c < ncol)
        return r, c, ok

    def halo(rc, bc):
        r, c, ok = place(rc, bc)
        there = SWAP[bc] * 3 + rc
        copy = pltpu.make_async_remote_copy(
            src_ref=image_ref, dst_ref=slots.at[there], send_sem=hsend.at[bc * 3 + rc],
            recv_sem=hrecv.at[there], device_id={"row": r, "col": c}, device_id_type=MESH,
        )
        return copy, ok

    order = [(1, 0), (2, 0), (0, 1), (0, 2), (1, 1), (1, 2), (2, 1), (2, 2)]
    for rc, bc in order:
        copy, ok = halo(rc, bc)

        @pl.when(ok)
        def _():
            copy.start()

    def step(s, carry):
        _, _, ok = place(lax.rem(s, 3), s // 3)

        @pl.when(ok)
        def _():
            @pl.when(s > 0)
            def _():
                pltpu.make_async_remote_copy(
                    src_ref=image_ref, dst_ref=slots.at[s], send_sem=hsend.at[s],
                    recv_sem=hrecv.at[s], device_id={"row": row, "col": col}, device_id_type=MESH,
                ).wait_recv()

            proj = mm(normed(slots[s]), fqkv_ref[:, width:])
            keys = cosine(proj[:, 0:width])
            kt[...] = keys.T.astype(BF)
            values = proj[:, width:]
            vext[0] = jnp.where(low, values, 1.0).astype(BF)
            vext[1] = jnp.where(low, 1.0, values).astype(BF)

            def block(i, c2):
                rows = pl.ds(pl.multiple_of(i * QB, QB), QB)
                s0 = mm(qs[0, rows, :], kt[...])
                s1 = mm(qs[1, rows, :], kt[...])
                p0 = jnp.exp2(s0).astype(BF)
                acc[0, rows, :] += mm(p0, vext[0])
                p1 = jnp.exp2(s1).astype(BF)
                acc[1, rows, :] += mm(p1, vext[1])
                return c2

            lax.fori_loop(0, tokens // QB, block, 0, unroll=2)

        return carry

    lax.fori_loop(0, 9, step, 0)

    for load in loads[5:]:
        load.wait()

    a0, a1 = acc[0], acc[1]
    num = jnp.where(low, a0, a1)
    den = pltpu.roll(jnp.where(low, a1, a0), HEAD, 1)
    attended = (num / den).astype(BF)
    branch = mm(attended, fout_ref[...])
    branch = branch * lax.rsqrt(jnp.mean(branch * branch, axis=-1, keepdims=True) + EPS)
    fine = (slots[0].astype(F32) + branch * fpost_ref[...]).astype(BF)
    fine_ref[...] = fine
    store = pltpu.make_async_copy(fine_ref, fine_hbm, local_sem.at[len(loads)])
    store.start()
    at = iota((64, tokens), 1)
    r, c = at // TILE, at % TILE
    span = 2 * POOL
    target = ((r % 2) * 2 + c % 2) * 16 + (r // span) * (TILE // span) + c // span
    pick = jnp.where(iota((64, tokens), 0) == target, 1.0, 0.0).astype(BF)
    sums = mm(pick, fine) * (1.0 / (POOL * POOL))
    high = sums.astype(BF)
    rest = (sums - high.astype(F32)).astype(BF)
    pooled = jnp.zeros((16, merge_w.shape[1]), F32)
    for p in range(4):
        part_w = merge_w[p * width : (p + 1) * width, :]
        pooled = pooled + mm(high[p * 16 : p * 16 + 16], part_w) + mm(rest[p * 16 : p * 16 + 16], part_w)
    coarse_in = mm(pooled.astype(BF), cin_w[...])
    cn = coarse_in * lax.rsqrt(jnp.mean(coarse_in * coarse_in, axis=-1, keepdims=True) + EPS) * coarse_gain
    quarter = coarse_in.shape[1] // 4
    for j in range(4):
        pack[4 * j : 4 * j + 4, :] = cn[0:4, j * quarter : (j + 1) * quarter]
    gath[me] = pack[...].astype(BF)

    def gather(i):
        peer = lax.rem(me + i, ndev)
        return pltpu.make_async_remote_copy(
            src_ref=gath.at[me], dst_ref=gath.at[me], send_sem=gsend.at[i], recv_sem=grecv.at[me],
            device_id={"row": peer // ncol, "col": lax.rem(peer, ncol)}, device_id_type=MESH,
        )

    def gather_from(i):
        peer = lax.rem(me + i, ndev)
        return pltpu.make_async_remote_copy(
            src_ref=gath.at[peer], dst_ref=gath.at[peer], send_sem=gsend.at[i],
            recv_sem=grecv.at[peer],
            device_id={"row": peer // ncol, "col": lax.rem(peer, ncol)}, device_id_type=MESH,
        )

    def loop(low_at, high_at, do):
        def one(i, carry):
            do(i)
            return carry

        lax.fori_loop(low_at, high_at, one, 0)

    loop(1, ndev, lambda i: gather(i).start())
    loop(1, ndev, lambda i: gather_from(i).wait_recv())

    every = gath[...].reshape(ndev * 16, quarter)
    lw = cqkv_w.shape[2]
    count = ndev * 4
    out_at, in_at = iota((count, ndev * 16), 0), iota((count, ndev * 16), 1)
    proj = [jnp.zeros((count, lw), F32) for _ in range(3)]
    for j in range(4):
        wanted = (out_at // 4) * 16 + j * 4 + out_at % 4
        chosen = mm(jnp.where(in_at == wanted, 1.0, 0.0).astype(BF), every).astype(BF)
        for k in range(3):
            proj[k] = proj[k] + mm(chosen, cqkv_w[k, j * quarter : (j + 1) * quarter, :])
    head_same = (iota((lw, lw), 0) // HEAD) == (iota((lw, lw), 1) // HEAD)
    head_ones = jnp.where(head_same, 1.0, 0.0)

    def ccosine(x):
        total = jnp.dot(x * x, head_ones, precision=HIGHEST)
        return x * lax.rsqrt(total * (1.0 / HEAD) + EPS)

    qall[...] = ccosine(proj[0])
    keys = ccosine(proj[1]).astype(BF)
    values = proj[2].astype(BF)
    own = ncol * 4
    queries = qall[pl.ds(pl.multiple_of(row * own, own), own), :]
    heads = lw // HEAD
    lane_head = iota((own, lw), 1) // HEAD
    stack = jnp.concatenate(
        [jnp.where(lane_head == h, queries, 0.0) for h in range(heads)], axis=0
    ).astype(BF)
    scores = lax.dot_general(stack, keys, (((1,), (1,)), ((), ())), preferred_element_type=F32)
    results = jnp.zeros((own, lw), F32)
    for h in range(heads):
        expo = jnp.exp(scores[h * own : (h + 1) * own] * (cscale_ref[h] / HEAD))
        weights = (expo / jnp.sum(expo, axis=-1, keepdims=True)).astype(BF)
        results = results + jnp.where(lane_head == h, mm(weights, values), 0.0)
    partial = mm(results.astype(BF), cout_w[...])
    for k in range(ncol):
        for j in range(4):
            pack[4 * j : 4 * j + 4, :] = partial[4 * k : 4 * k + 4, j * quarter : (j + 1) * quarter]
        sbuf[k] = pack[...].astype(BF)
    rbuf[col] = sbuf[col]

    def reduce(i):
        peer = lax.rem(col + i, ncol)
        return pltpu.make_async_remote_copy(
            src_ref=sbuf.at[peer], dst_ref=rbuf.at[col], send_sem=rsend.at[i],
            recv_sem=rrecv.at[col], device_id={"row": row, "col": peer}, device_id_type=MESH,
        )

    def reduce_from(i):
        peer = lax.rem(col + i, ncol)
        return pltpu.make_async_remote_copy(
            src_ref=sbuf.at[peer], dst_ref=rbuf.at[peer], send_sem=rsend.at[i],
            recv_sem=rrecv.at[peer], device_id={"row": row, "col": peer}, device_id_type=MESH,
        )

    loop(1, ncol, lambda i: reduce(i).start())
    loop(1, ncol, lambda i: reduce_from(i).wait_recv())
    total = jnp.sum(rbuf[...].astype(F32), axis=0)
    pack[...] = total
    pieces = [pack[4 * j : 4 * j + 4, :] for j in range(4)]
    power = sum(jnp.sum(piece * piece, axis=-1, keepdims=True) for piece in pieces)
    inverse = lax.rsqrt(power * (1.0 / (4 * quarter)) + EPS)
    for j in range(4):
        at_j = slice(j * quarter, (j + 1) * quarter)
        y = coarse_in[0:4, at_j] + pieces[j] * inverse * cpost_ref[:, at_j]
        for k in range(coarse_ref.shape[0]):
            side = coarse_ref.shape[1]
            coarse_ref[k, :, at_j] = y[k * side : (k + 1) * side].astype(BF)

    store.wait()

    for rc, bc in order:
        copy, ok = halo(rc, bc)

        @pl.when(ok)
        def _():
            copy.wait_send()

    loop(1, ndev, lambda i: gather(i).wait_send())
    loop(1, ncol, lambda i: reduce(i).wait_send())


def body(
    image, noise_level, cond_table, ada_fine, fine_qkv, fine_scale, fine_out_w, fine_post,
    merge_w, coarse_in_w, ada_coarse, coarse_qkv, coarse_scale, coarse_out_w, coarse_post,
):
    nrow, ncol = lax.axis_size("row"), lax.axis_size("col")
    ndev = nrow * ncol
    rows, cols, width = image.shape
    tokens = rows * cols
    lw = coarse_qkv.shape[2]
    cw = coarse_in_w.shape[1]
    quarter = cw // 4
    side = TILE // (2 * POOL)
    smem = pl.BlockSpec(memory_space=pltpu.SMEM)
    vmem = pl.BlockSpec(memory_space=pltpu.VMEM)
    hbm = pl.BlockSpec(memory_space=pl.ANY)
    dma = pltpu.SemaphoreType.DMA
    fine, coarse = pl.pallas_call(
        functools.partial(kernel, nrow, ncol),
        out_shape=(
            jax.ShapeDtypeStruct((tokens, width), BF),
            jax.ShapeDtypeStruct((side, side, cw), BF),
        ),
        in_specs=[smem] * 3 + [hbm] * 12,
        out_specs=(hbm, vmem),
        scratch_shapes=[
            pltpu.VMEM((9, tokens, width), BF),
            pltpu.VMEM((2, tokens, width), BF),
            pltpu.VMEM((width, tokens), BF),
            pltpu.VMEM((2, tokens, width), BF),
            pltpu.VMEM((2, tokens, width), F32),
            pltpu.VMEM(cond_table.shape, F32),
            pltpu.VMEM(ada_fine.shape, F32),
            pltpu.VMEM(fine_qkv.shape, BF),
            pltpu.VMEM(fine_out_w.shape, BF),
            pltpu.VMEM((1, width), F32),
            pltpu.VMEM((1, cw), F32),
            pltpu.VMEM(merge_w.shape, BF),
            pltpu.VMEM(coarse_in_w.shape, BF),
            pltpu.VMEM(ada_coarse.shape, F32),
            pltpu.VMEM(coarse_qkv.shape, BF),
            pltpu.VMEM(coarse_out_w.shape, BF),
            pltpu.VMEM((tokens, width), BF),
            pltpu.VMEM((ndev, 16, quarter), BF),
            pltpu.VMEM((16, quarter), F32),
            pltpu.VMEM((ndev * 4, lw), F32),
            pltpu.VMEM((ncol, 16, quarter), BF),
            pltpu.VMEM((ncol, 16, quarter), BF),
            dma((13,)), dma((9,)), dma((9,)), dma((ndev,)), dma((ndev,)), dma((ncol,)), dma((ncol,)),
        ],
        compiler_params=pltpu.CompilerParams(
            collective_id=0, has_side_effects=True, vmem_limit_bytes=VMEM_BYTES
        ),
        cost_estimate=pl.CostEstimate(
            flops=tokens * tokens * 9 * width * 4, bytes_accessed=8 << 20,
            transcendentals=tokens * tokens * 18,
        ),
    )(
        noise_level, fine_scale, coarse_scale, image.reshape(tokens, width), cond_table, ada_fine,
        fine_qkv, fine_out_w, fine_post.reshape(1, -1), coarse_post.reshape(1, -1), merge_w,
        coarse_in_w, ada_coarse, coarse_qkv, coarse_out_w,
    )
    return fine.reshape(rows, cols, width), coarse


def solution(mesh):
    in_specs = (
        P(("noise", "row"), "col", None),
        P("noise"),
        P(),
        P(),
        P(),
        P(),
        P(),
        P(),
        P(),
        P(),
        P(),
        P(None, None, "col"),
        P("col"),
        P("col", None),
        P(),
    )
    out_specs = (P(("noise", "row"), "col", None), P(("noise", "row"), "col", None))
    return jax.shard_map(body, mesh=mesh, in_specs=in_specs, out_specs=out_specs, check_vma=False)
```

```python
import functools
import math

import jax
import jax.numpy as jnp
from jax import lax
from jax.experimental import pallas as pl
from jax.experimental.pallas import tpu as pltpu
from jax.sharding import PartitionSpec as P

HEAD = 64
TILE = 32
POOL = 8
KB = 256
VMEM_BYTES = 64 * 1024 * 1024 - 65536
EPS = 1e-6
MESH = pl.DeviceIdType.MESH
HIGHEST = lax.Precision.HIGHEST
BF = jnp.bfloat16
F32 = jnp.float32
SWAP = (0, 2, 1)


def mm(a, b):
    return jnp.dot(a, b, preferred_element_type=F32)


def iota(shape, dim):
    return lax.broadcasted_iota(jnp.int32, shape, dim)


def kernel(
    nrow, ncol, level_ref, fscale_ref, cscale_ref, image_hbm, table_hbm, adaf_hbm, fqkv_hbm,
    fout_hbm, fpost_hbm, cpost_hbm, merge_hbm, cin_hbm, adac_hbm, cqkv_hbm, cout_hbm,
    fine_hbm, coarse_ref,
    slots, qs, kt, vext, acc, table_ref, ada_fine_ref, fqkv_ref, fout_ref, fpost_ref, cpost_ref,
    merge_w, cin_w, adac_w, cqkv_w, cout_w, fine_ref, gath, pack, qall,
    sbuf, rbuf, local_sem, hsend, hrecv, gsend, grecv, rsend, rrecv,
):
    tokens, width = image_hbm.shape
    image_ref = slots.at[0]
    ndev = nrow * ncol
    row, col = lax.axis_index("row"), lax.axis_index("col")
    me = row * ncol + col
    sib = 1 - 2 * lax.rem(row, 2)

    loads = [
        pltpu.make_async_copy(src, dst, local_sem.at[i])
        for i, (src, dst) in enumerate(
            ((image_hbm, image_ref), (table_hbm, table_ref), (adaf_hbm, ada_fine_ref),
             (fqkv_hbm, fqkv_ref), (adac_hbm, adac_w), (fout_hbm, fout_ref),
             (fpost_hbm, fpost_ref), (cpost_hbm, cpost_ref), (merge_hbm, merge_w),
             (cin_hbm, cin_w), (cqkv_hbm, cqkv_w), (cout_hbm, cout_w))
        )
    ]
    for load in loads:
        load.start()

    barrier = pltpu.get_barrier_semaphore()

    def greet(i, carry):
        peer = lax.rem(me + i, ndev)
        pl.semaphore_signal(
            barrier, inc=1, device_id={"row": peer // ncol, "col": lax.rem(peer, ncol)},
            device_id_type=MESH,
        )
        return carry

    lax.fori_loop(1, ndev, greet, 0)
    for load in loads[:4]:
        load.wait()
    levels = table_ref.shape[0]
    hot = iota((levels, 1), 0) == level_ref[0]
    cond = jnp.sum(jnp.where(hot, table_ref[...], 0.0), axis=0, keepdims=True)
    cond = jnp.broadcast_to(cond, (8, cond.shape[1]))
    fine_gain = 1.0 + jnp.dot(cond, ada_fine_ref[...], precision=HIGHEST)[0:1]
    low = iota((1, width), 1) < HEAD
    same = (iota((width, width), 0) // HEAD) == (iota((width, width), 1) // HEAD)
    block_ones = jnp.where(same, 1.0, 0.0).astype(BF)

    all_ones = jnp.ones((width, width), BF)

    def normed(x):
        x = x.astype(F32)
        total = mm((x * x).astype(BF), all_ones)
        return (x * lax.rsqrt(total * (1.0 / width) + EPS) * fine_gain).astype(BF)

    def cosine(x):
        total = mm((x * x).astype(BF), block_ones)
        return x * lax.rsqrt(total * (1.0 / HEAD) + EPS)

    factor = math.log2(math.e) / HEAD
    qscale = jnp.where(low, fscale_ref[0] * factor, fscale_ref[1] * factor)
    queries = cosine(mm(normed(slots[0]), fqkv_ref[:, 0:width])) * qscale
    qs[0] = jnp.where(low, queries, 0.0).astype(BF)
    qs[1] = jnp.where(low, 0.0, queries).astype(BF)
    acc[...] = jnp.zeros_like(acc)
    loads[4].wait()
    coarse_gain = 1.0 + jnp.dot(cond, adac_w[...], precision=HIGHEST)[0:1]

    pl.semaphore_wait(barrier, ndev - 1)

    def place(rc, bc):
        a = jnp.where(rc == 0, 0, jnp.where(rc == 1, sib, -sib))
        b = jnp.where(bc == 0, 0, jnp.where(bc == 1, -1, 1))
        r, c = row + a, col + b
        ok = (r >= 0) & (r < nrow) & (c >= 0) & (c < ncol)
        return r, c, ok

    def halo(rc, bc):
        r, c, ok = place(rc, bc)
        there = SWAP[bc] * 3 + rc
        copy = pltpu.make_async_remote_copy(
            src_ref=image_ref, dst_ref=slots.at[there], send_sem=hsend.at[bc * 3 + rc],
            recv_sem=hrecv.at[there], device_id={"row": r, "col": c}, device_id_type=MESH,
        )
        return copy, ok

    order = [(1, 0), (2, 0), (0, 1), (0, 2), (1, 1), (1, 2), (2, 1), (2, 2)]
    for rc, bc in order:
        copy, ok = halo(rc, bc)

        @pl.when(ok)
        def _():
            copy.start()

    def step(s, carry):
        _, _, ok = place(lax.rem(s, 3), s // 3)

        @pl.when(ok)
        def _():
            @pl.when(s > 0)
            def _():
                pltpu.make_async_remote_copy(
                    src_ref=image_ref, dst_ref=slots.at[s], send_sem=hsend.at[s],
                    recv_sem=hrecv.at[s], device_id={"row": row, "col": col}, device_id_type=MESH,
                ).wait_recv()

            proj = mm(normed(slots[s]), fqkv_ref[:, width:])
            keys = cosine(proj[:, 0:width])
            for i in range(tokens // KB):
                kt[i] = keys[i * KB : (i + 1) * KB].T.astype(BF)
            values = proj[:, width:]
            vext[0] = jnp.where(low, values, 1.0).astype(BF)
            vext[1] = jnp.where(low, 1.0, values).astype(BF)

            def block(i, c2):
                keys_at = pl.ds(pl.multiple_of(i * KB, KB), KB)
                for head in range(2):
                    scores = mm(qs[head], kt[i])
                    expo = jnp.exp2(scores).astype(BF)
                    acc[head] += mm(expo, vext[head, keys_at, :])
                return c2

            lax.fori_loop(0, tokens // KB, block, 0)

        return carry

    lax.fori_loop(0, 9, step, 0)

    for load in loads[5:]:
        load.wait()

    a0, a1 = acc[0], acc[1]
    num = jnp.where(low, a0, a1)
    den = pltpu.roll(jnp.where(low, a1, a0), HEAD, 1)
    attended = (num / den).astype(BF)
    branch = mm(attended, fout_ref[...])
    branch = branch * lax.rsqrt(jnp.mean(branch * branch, axis=-1, keepdims=True) + EPS)
    fine = (slots[0].astype(F32) + branch * fpost_ref[...]).astype(BF)
    fine_ref[...] = fine
    store = pltpu.make_async_copy(fine_ref, fine_hbm, local_sem.at[len(loads)])
    store.start()
    at = iota((64, tokens), 1)
    r, c = at // TILE, at % TILE
    span = 2 * POOL
    target = ((r % 2) * 2 + c % 2) * 16 + (r // span) * (TILE // span) + c // span
    pick = jnp.where(iota((64, tokens), 0) == target, 1.0, 0.0).astype(BF)
    sums = mm(pick, fine) * (1.0 / (POOL * POOL))
    high = sums.astype(BF)
    rest = (sums - high.astype(F32)).astype(BF)
    pooled = jnp.zeros((16, merge_w.shape[1]), F32)
    for p in range(4):
        part_w = merge_w[p * width : (p + 1) * width, :]
        pooled = pooled + mm(high[p * 16 : p * 16 + 16], part_w) + mm(rest[p * 16 : p * 16 + 16], part_w)
    coarse_in = mm(pooled.astype(BF), cin_w[...])
    cn = coarse_in * lax.rsqrt(jnp.mean(coarse_in * coarse_in, axis=-1, keepdims=True) + EPS) * coarse_gain
    quarter = coarse_in.shape[1] // 4
    for j in range(4):
        pack[4 * j : 4 * j + 4, :] = cn[0:4, j * quarter : (j + 1) * quarter]
    gath[me] = pack[...].astype(BF)

    def gather(i):
        peer = lax.rem(me + i, ndev)
        return pltpu.make_async_remote_copy(
            src_ref=gath.at[me], dst_ref=gath.at[me], send_sem=gsend.at[i], recv_sem=grecv.at[me],
            device_id={"row": peer // ncol, "col": lax.rem(peer, ncol)}, device_id_type=MESH,
        )

    def gather_from(i):
        peer = lax.rem(me + i, ndev)
        return pltpu.make_async_remote_copy(
            src_ref=gath.at[peer], dst_ref=gath.at[peer], send_sem=gsend.at[i],
            recv_sem=grecv.at[peer],
            device_id={"row": peer // ncol, "col": lax.rem(peer, ncol)}, device_id_type=MESH,
        )

    def loop(low_at, high_at, do):
        def one(i, carry):
            do(i)
            return carry

        lax.fori_loop(low_at, high_at, one, 0)

    loop(1, ndev, lambda i: gather(i).start())
    loop(1, ndev, lambda i: gather_from(i).wait_recv())

    every = gath[...].reshape(ndev * 16, quarter)
    lw = cqkv_w.shape[2]
    count = ndev * 4
    out_at, in_at = iota((count, ndev * 16), 0), iota((count, ndev * 16), 1)
    proj = [jnp.zeros((count, lw), F32) for _ in range(3)]
    for j in range(4):
        wanted = (out_at // 4) * 16 + j * 4 + out_at % 4
        chosen = mm(jnp.where(in_at == wanted, 1.0, 0.0).astype(BF), every).astype(BF)
        for k in range(3):
            proj[k] = proj[k] + mm(chosen, cqkv_w[k, j * quarter : (j + 1) * quarter, :])
    head_same = (iota((lw, lw), 0) // HEAD) == (iota((lw, lw), 1) // HEAD)
    head_ones = jnp.where(head_same, 1.0, 0.0)

    def ccosine(x):
        total = jnp.dot(x * x, head_ones, precision=HIGHEST)
        return x * lax.rsqrt(total * (1.0 / HEAD) + EPS)

    qall[...] = ccosine(proj[0])
    keys = ccosine(proj[1]).astype(BF)
    values = proj[2].astype(BF)
    own = ncol * 4
    queries = qall[pl.ds(pl.multiple_of(row * own, own), own), :]
    heads = lw // HEAD
    lane_head = iota((own, lw), 1) // HEAD
    stack = jnp.concatenate(
        [jnp.where(lane_head == h, queries, 0.0) for h in range(heads)], axis=0
    ).astype(BF)
    scores = lax.dot_general(stack, keys, (((1,), (1,)), ((), ())), preferred_element_type=F32)
    results = jnp.zeros((own, lw), F32)
    for h in range(heads):
        expo = jnp.exp(scores[h * own : (h + 1) * own] * (cscale_ref[h] / HEAD))
        weights = (expo / jnp.sum(expo, axis=-1, keepdims=True)).astype(BF)
        results = results + jnp.where(lane_head == h, mm(weights, values), 0.0)
    partial = mm(results.astype(BF), cout_w[...])
    for k in range(ncol):
        for j in range(4):
            pack[4 * j : 4 * j + 4, :] = partial[4 * k : 4 * k + 4, j * quarter : (j + 1) * quarter]
        sbuf[k] = pack[...].astype(BF)
    rbuf[col] = sbuf[col]

    def reduce(i):
        peer = lax.rem(col + i, ncol)
        return pltpu.make_async_remote_copy(
            src_ref=sbuf.at[peer], dst_ref=rbuf.at[col], send_sem=rsend.at[i],
            recv_sem=rrecv.at[col], device_id={"row": row, "col": peer}, device_id_type=MESH,
        )

    def reduce_from(i):
        peer = lax.rem(col + i, ncol)
        return pltpu.make_async_remote_copy(
            src_ref=sbuf.at[peer], dst_ref=rbuf.at[peer], send_sem=rsend.at[i],
            recv_sem=rrecv.at[peer], device_id={"row": row, "col": peer}, device_id_type=MESH,
        )

    loop(1, ncol, lambda i: reduce(i).start())
    loop(1, ncol, lambda i: reduce_from(i).wait_recv())
    total = jnp.sum(rbuf[...].astype(F32), axis=0)
    pack[...] = total
    pieces = [pack[4 * j : 4 * j + 4, :] for j in range(4)]
    power = sum(jnp.sum(piece * piece, axis=-1, keepdims=True) for piece in pieces)
    inverse = lax.rsqrt(power * (1.0 / (4 * quarter)) + EPS)
    for j in range(4):
        at_j = slice(j * quarter, (j + 1) * quarter)
        y = coarse_in[0:4, at_j] + pieces[j] * inverse * cpost_ref[:, at_j]
        for k in range(coarse_ref.shape[0]):
            side = coarse_ref.shape[1]
            coarse_ref[k, :, at_j] = y[k * side : (k + 1) * side].astype(BF)

    store.wait()

    for rc, bc in order:
        copy, ok = halo(rc, bc)

        @pl.when(ok)
        def _():
            copy.wait_send()

    loop(1, ndev, lambda i: gather(i).wait_send())
    loop(1, ncol, lambda i: reduce(i).wait_send())


def writer(fine_ref, coarse_ref, fine_out_ref, coarse_out_ref, sem):
    copies = [
        pltpu.make_async_copy(fine_ref, fine_out_ref, sem.at[0]),
        pltpu.make_async_copy(coarse_ref, coarse_out_ref, sem.at[1]),
    ]
    for copy in copies:
        copy.start()
    for copy in copies:
        copy.wait()


def body(
    image, noise_level, cond_table, ada_fine, fine_qkv, fine_scale, fine_out_w, fine_post,
    merge_w, coarse_in_w, ada_coarse, coarse_qkv, coarse_scale, coarse_out_w, coarse_post,
):
    nrow, ncol = lax.axis_size("row"), lax.axis_size("col")
    ndev = nrow * ncol
    rows, cols, width = image.shape
    tokens = rows * cols
    lw = coarse_qkv.shape[2]
    cw = coarse_in_w.shape[1]
    quarter = cw // 4
    side = TILE // (2 * POOL)
    smem = pl.BlockSpec(memory_space=pltpu.SMEM)
    vmem = pl.BlockSpec(memory_space=pltpu.VMEM)
    hbm = pl.BlockSpec(memory_space=pl.ANY)
    dma = pltpu.SemaphoreType.DMA
    fine, coarse = pl.pallas_call(
        functools.partial(kernel, nrow, ncol),
        out_shape=(
            jax.ShapeDtypeStruct((tokens, width), BF),
            jax.ShapeDtypeStruct((side, side, cw), BF),
        ),
        in_specs=[smem] * 3 + [hbm] * 12,
        out_specs=(hbm, vmem),
        scratch_shapes=[
            pltpu.VMEM((9, tokens, width), BF),
            pltpu.VMEM((2, tokens, width), BF),
            pltpu.VMEM((tokens // KB, width, KB), BF),
            pltpu.VMEM((2, tokens, width), BF),
            pltpu.VMEM((2, tokens, width), F32),
            pltpu.VMEM(cond_table.shape, F32),
            pltpu.VMEM(ada_fine.shape, F32),
            pltpu.VMEM(fine_qkv.shape, BF),
            pltpu.VMEM(fine_out_w.shape, BF),
            pltpu.VMEM((1, width), F32),
            pltpu.VMEM((1, cw), F32),
            pltpu.VMEM(merge_w.shape, BF),
            pltpu.VMEM(coarse_in_w.shape, BF),
            pltpu.VMEM(ada_coarse.shape, F32),
            pltpu.VMEM(coarse_qkv.shape, BF),
            pltpu.VMEM(coarse_out_w.shape, BF),
            pltpu.VMEM((tokens, width), BF),
            pltpu.VMEM((ndev, 16, quarter), BF),
            pltpu.VMEM((16, quarter), F32),
            pltpu.VMEM((ndev * 4, lw), F32),
            pltpu.VMEM((ncol, 16, quarter), BF),
            pltpu.VMEM((ncol, 16, quarter), BF),
            dma((13,)), dma((9,)), dma((9,)), dma((ndev,)), dma((ndev,)), dma((ncol,)), dma((ncol,)),
        ],
        compiler_params=pltpu.CompilerParams(
            collective_id=0, has_side_effects=True, vmem_limit_bytes=VMEM_BYTES
        ),
        cost_estimate=pl.CostEstimate(
            flops=tokens * tokens * 9 * width * 4, bytes_accessed=8 << 20,
            transcendentals=tokens * tokens * 18,
        ),
    )(
        noise_level, fine_scale, coarse_scale, image.reshape(tokens, width), cond_table, ada_fine,
        fine_qkv, fine_out_w, fine_post.reshape(1, -1), coarse_post.reshape(1, -1), merge_w,
        coarse_in_w, ada_coarse, coarse_qkv, coarse_out_w,
    )
    fine, coarse = pl.pallas_call(
        writer,
        out_shape=(
            jax.ShapeDtypeStruct(fine.shape, BF),
            jax.ShapeDtypeStruct(coarse.shape, BF),
        ),
        in_specs=[hbm, hbm],
        out_specs=(hbm, hbm),
        scratch_shapes=[dma((2,))],
        compiler_params=pltpu.CompilerParams(vmem_limit_bytes=VMEM_BYTES),
    )(fine, coarse)
    return fine.reshape(rows, cols, width), coarse


def solution(mesh):
    in_specs = (
        P(("noise", "row"), "col", None),
        P("noise"),
        P(),
        P(),
        P(),
        P(),
        P(),
        P(),
        P(),
        P(),
        P(),
        P(None, None, "col"),
        P("col"),
        P("col", None),
        P(),
    )
    out_specs = (P(("noise", "row"), "col", None), P(("noise", "row"), "col", None))
    return jax.shard_map(body, mesh=mesh, in_specs=in_specs, out_specs=out_specs, check_vma=False)
```

```python
import functools
import math

import jax
import jax.numpy as jnp
from jax import lax
from jax.experimental import pallas as pl
from jax.experimental.pallas import tpu as pltpu
from jax.sharding import PartitionSpec as P

HEAD = 64
TILE = 32
POOL = 8
KB = 256
QB = 256
ROWS = HEAD + 16
VMEM_BYTES = 64 * 1024 * 1024 - 65536
EPS = 1e-6
MESH = pl.DeviceIdType.MESH
HIGHEST = lax.Precision.HIGHEST
BF = jnp.bfloat16
F32 = jnp.float32
SWAP = (0, 2, 1)


def mm(a, b):
    return jnp.dot(a, b, preferred_element_type=F32)


def iota(shape, dim):
    return lax.broadcasted_iota(jnp.int32, shape, dim)


def kernel(
    nrow, ncol, level_ref, fscale_ref, cscale_ref, image_hbm, table_hbm, adaf_hbm, fqkv_hbm,
    fout_hbm, fpost_hbm, cpost_hbm, merge_hbm, cin_hbm, adac_hbm, cqkv_hbm, cout_hbm,
    fine_hbm, coarse_ref,
    slots, qs, kt, vext, acc, table_ref, ada_fine_ref, fqkv_ref, fout_ref, fpost_ref, cpost_ref,
    merge_w, cin_w, adac_w, cqkv_w, cout_w, fine_ref, gath, pack, qall,
    sbuf, rbuf, local_sem, hsend, hrecv, gsend, grecv, rsend, rrecv,
):
    tokens, width = image_hbm.shape
    image_ref = slots.at[0]
    ndev = nrow * ncol
    row, col = lax.axis_index("row"), lax.axis_index("col")
    me = row * ncol + col
    sib = 1 - 2 * lax.rem(row, 2)

    loads = [
        pltpu.make_async_copy(src, dst, local_sem.at[i])
        for i, (src, dst) in enumerate(
            ((image_hbm, image_ref), (table_hbm, table_ref), (adaf_hbm, ada_fine_ref),
             (fqkv_hbm, fqkv_ref), (adac_hbm, adac_w), (fout_hbm, fout_ref),
             (fpost_hbm, fpost_ref), (cpost_hbm, cpost_ref), (merge_hbm, merge_w),
             (cin_hbm, cin_w), (cqkv_hbm, cqkv_w), (cout_hbm, cout_w))
        )
    ]
    for load in loads:
        load.start()

    barrier = pltpu.get_barrier_semaphore()

    def greet(i, carry):
        peer = lax.rem(me + i, ndev)
        pl.semaphore_signal(
            barrier, inc=1, device_id={"row": peer // ncol, "col": lax.rem(peer, ncol)},
            device_id_type=MESH,
        )
        return carry

    lax.fori_loop(1, ndev, greet, 0)
    for load in loads[:4]:
        load.wait()
    levels = table_ref.shape[0]
    hot = iota((levels, 1), 0) == level_ref[0]
    cond = jnp.sum(jnp.where(hot, table_ref[...], 0.0), axis=0, keepdims=True)
    cond = jnp.broadcast_to(cond, (8, cond.shape[1]))
    fine_gain = 1.0 + jnp.dot(cond, ada_fine_ref[...], precision=HIGHEST)[0:1]
    low = iota((1, width), 1) < HEAD
    same = (iota((width, width), 0) // HEAD) == (iota((width, width), 1) // HEAD)
    block_ones = jnp.where(same, 1.0, 0.0).astype(BF)

    all_ones = jnp.ones((width, width), BF)

    def normed(x):
        x = x.astype(F32)
        total = mm((x * x).astype(BF), all_ones)
        return (x * lax.rsqrt(total * (1.0 / width) + EPS) * fine_gain).astype(BF)

    def cosine(x):
        total = mm((x * x).astype(BF), block_ones)
        return x * lax.rsqrt(total * (1.0 / HEAD) + EPS)

    factor = math.log2(math.e) / HEAD
    qscale = jnp.where(low, fscale_ref[0] * factor, fscale_ref[1] * factor)
    queries = cosine(mm(normed(slots[0]), fqkv_ref[:, 0:width])) * qscale
    first = iota((width, 1), 0) < HEAD
    for i in range(tokens // QB):
        part = queries[i * QB : (i + 1) * QB].T
        qs[0, i] = jnp.where(first, part, 0.0).astype(BF)
        qs[1, i] = jnp.where(first, 0.0, part).astype(BF)
    vext[...] = jnp.ones_like(vext)
    acc[...] = jnp.zeros_like(acc)
    loads[4].wait()
    coarse_gain = 1.0 + jnp.dot(cond, adac_w[...], precision=HIGHEST)[0:1]

    pl.semaphore_wait(barrier, ndev - 1)

    def place(rc, bc):
        a = jnp.where(rc == 0, 0, jnp.where(rc == 1, sib, -sib))
        b = jnp.where(bc == 0, 0, jnp.where(bc == 1, -1, 1))
        r, c = row + a, col + b
        ok = (r >= 0) & (r < nrow) & (c >= 0) & (c < ncol)
        return r, c, ok

    def halo(rc, bc):
        r, c, ok = place(rc, bc)
        there = SWAP[bc] * 3 + rc
        copy = pltpu.make_async_remote_copy(
            src_ref=image_ref, dst_ref=slots.at[there], send_sem=hsend.at[bc * 3 + rc],
            recv_sem=hrecv.at[there], device_id={"row": r, "col": c}, device_id_type=MESH,
        )
        return copy, ok

    order = [(1, 0), (2, 0), (0, 1), (0, 2), (1, 1), (1, 2), (2, 1), (2, 2)]
    for rc, bc in order:
        copy, ok = halo(rc, bc)

        @pl.when(ok)
        def _():
            copy.start()

    def step(s, carry):
        _, _, ok = place(lax.rem(s, 3), s // 3)

        @pl.when(ok)
        def _():
            @pl.when(s > 0)
            def _():
                pltpu.make_async_remote_copy(
                    src_ref=image_ref, dst_ref=slots.at[s], send_sem=hsend.at[s],
                    recv_sem=hrecv.at[s], device_id={"row": row, "col": col}, device_id_type=MESH,
                ).wait_recv()

            proj = mm(normed(slots[s]), fqkv_ref[:, width:])
            kt[...] = cosine(proj[:, 0:width]).astype(BF)
            for i in range(tokens // KB):
                at_i = slice(i * KB, (i + 1) * KB)
                part = proj[at_i, width:].T.astype(BF)
                for head in range(2):
                    vext[head, 0:HEAD, at_i] = part[head * HEAD : (head + 1) * HEAD]

            def block(i, c2):
                for head in range(2):
                    total = acc[head, i]
                    for j in range(tokens // KB):
                        at_j = slice(j * KB, (j + 1) * KB)
                        expo = jnp.exp2(mm(kt[at_j], qs[head, i])).astype(BF)
                        total = total + mm(vext[head, :, at_j], expo)
                    acc[head, i] = total
                return c2

            lax.fori_loop(0, tokens // QB, block, 0)

        return carry

    lax.fori_loop(0, 9, step, 0)

    for load in loads[5:]:
        load.wait()

    parts = []
    for i in range(tokens // QB):
        ratio = [acc[head, i, 0:HEAD] / acc[head, i, HEAD : HEAD + 1] for head in range(2)]
        parts.append(jnp.concatenate(ratio, axis=0).T.astype(BF))
    attended = jnp.concatenate(parts, axis=0)
    branch = mm(attended, fout_ref[...])
    branch = branch * lax.rsqrt(jnp.mean(branch * branch, axis=-1, keepdims=True) + EPS)
    fine = (slots[0].astype(F32) + branch * fpost_ref[...]).astype(BF)
    fine_ref[...] = fine
    store = pltpu.make_async_copy(fine_ref, fine_hbm, local_sem.at[len(loads)])
    store.start()
    at = iota((64, tokens), 1)
    r, c = at // TILE, at % TILE
    span = 2 * POOL
    target = ((r % 2) * 2 + c % 2) * 16 + (r // span) * (TILE // span) + c // span
    pick = jnp.where(iota((64, tokens), 0) == target, 1.0, 0.0).astype(BF)
    sums = mm(pick, fine) * (1.0 / (POOL * POOL))
    high = sums.astype(BF)
    rest = (sums - high.astype(F32)).astype(BF)
    pooled = jnp.zeros((16, merge_w.shape[1]), F32)
    for p in range(4):
        part_w = merge_w[p * width : (p + 1) * width, :]
        pooled = pooled + mm(high[p * 16 : p * 16 + 16], part_w) + mm(rest[p * 16 : p * 16 + 16], part_w)
    coarse_in = mm(pooled.astype(BF), cin_w[...])
    cn = coarse_in * lax.rsqrt(jnp.mean(coarse_in * coarse_in, axis=-1, keepdims=True) + EPS) * coarse_gain
    quarter = coarse_in.shape[1] // 4
    for j in range(4):
        pack[4 * j : 4 * j + 4, :] = cn[0:4, j * quarter : (j + 1) * quarter]
    gath[me] = pack[...].astype(BF)

    def gather(i):
        peer = lax.rem(me + i, ndev)
        return pltpu.make_async_remote_copy(
            src_ref=gath.at[me], dst_ref=gath.at[me], send_sem=gsend.at[i], recv_sem=grecv.at[me],
            device_id={"row": peer // ncol, "col": lax.rem(peer, ncol)}, device_id_type=MESH,
        )

    def gather_from(i):
        peer = lax.rem(me + i, ndev)
        return pltpu.make_async_remote_copy(
            src_ref=gath.at[peer], dst_ref=gath.at[peer], send_sem=gsend.at[i],
            recv_sem=grecv.at[peer],
            device_id={"row": peer // ncol, "col": lax.rem(peer, ncol)}, device_id_type=MESH,
        )

    def loop(low_at, high_at, do):
        def one(i, carry):
            do(i)
            return carry

        lax.fori_loop(low_at, high_at, one, 0)

    loop(1, ndev, lambda i: gather(i).start())
    loop(1, ndev, lambda i: gather_from(i).wait_recv())

    every = gath[...].reshape(ndev * 16, quarter)
    lw = cqkv_w.shape[2]
    count = ndev * 4
    out_at, in_at = iota((count, ndev * 16), 0), iota((count, ndev * 16), 1)
    proj = [jnp.zeros((count, lw), F32) for _ in range(3)]
    for j in range(4):
        wanted = (out_at // 4) * 16 + j * 4 + out_at % 4
        chosen = mm(jnp.where(in_at == wanted, 1.0, 0.0).astype(BF), every).astype(BF)
        for k in range(3):
            proj[k] = proj[k] + mm(chosen, cqkv_w[k, j * quarter : (j + 1) * quarter, :])
    head_same = (iota((lw, lw), 0) // HEAD) == (iota((lw, lw), 1) // HEAD)
    head_ones = jnp.where(head_same, 1.0, 0.0)

    def ccosine(x):
        total = jnp.dot(x * x, head_ones, precision=HIGHEST)
        return x * lax.rsqrt(total * (1.0 / HEAD) + EPS)

    qall[...] = ccosine(proj[0])
    keys = ccosine(proj[1]).astype(BF)
    values = proj[2].astype(BF)
    own = ncol * 4
    queries = qall[pl.ds(pl.multiple_of(row * own, own), own), :]
    heads = lw // HEAD
    lane_head = iota((own, lw), 1) // HEAD
    stack = jnp.concatenate(
        [jnp.where(lane_head == h, queries, 0.0) for h in range(heads)], axis=0
    ).astype(BF)
    scores = lax.dot_general(stack, keys, (((1,), (1,)), ((), ())), preferred_element_type=F32)
    results = jnp.zeros((own, lw), F32)
    for h in range(heads):
        expo = jnp.exp(scores[h * own : (h + 1) * own] * (cscale_ref[h] / HEAD))
        weights = (expo / jnp.sum(expo, axis=-1, keepdims=True)).astype(BF)
        results = results + jnp.where(lane_head == h, mm(weights, values), 0.0)
    partial = mm(results.astype(BF), cout_w[...])
    for k in range(ncol):
        for j in range(4):
            pack[4 * j : 4 * j + 4, :] = partial[4 * k : 4 * k + 4, j * quarter : (j + 1) * quarter]
        sbuf[k] = pack[...].astype(BF)
    rbuf[col] = sbuf[col]

    def reduce(i):
        peer = lax.rem(col + i, ncol)
        return pltpu.make_async_remote_copy(
            src_ref=sbuf.at[peer], dst_ref=rbuf.at[col], send_sem=rsend.at[i],
            recv_sem=rrecv.at[col], device_id={"row": row, "col": peer}, device_id_type=MESH,
        )

    def reduce_from(i):
        peer = lax.rem(col + i, ncol)
        return pltpu.make_async_remote_copy(
            src_ref=sbuf.at[peer], dst_ref=rbuf.at[peer], send_sem=rsend.at[i],
            recv_sem=rrecv.at[peer], device_id={"row": row, "col": peer}, device_id_type=MESH,
        )

    loop(1, ncol, lambda i: reduce(i).start())
    loop(1, ncol, lambda i: reduce_from(i).wait_recv())
    total = jnp.sum(rbuf[...].astype(F32), axis=0)
    pack[...] = total
    pieces = [pack[4 * j : 4 * j + 4, :] for j in range(4)]
    power = sum(jnp.sum(piece * piece, axis=-1, keepdims=True) for piece in pieces)
    inverse = lax.rsqrt(power * (1.0 / (4 * quarter)) + EPS)
    for j in range(4):
        at_j = slice(j * quarter, (j + 1) * quarter)
        y = coarse_in[0:4, at_j] + pieces[j] * inverse * cpost_ref[:, at_j]
        for k in range(coarse_ref.shape[0]):
            side = coarse_ref.shape[1]
            coarse_ref[k, :, at_j] = y[k * side : (k + 1) * side].astype(BF)

    store.wait()

    for rc, bc in order:
        copy, ok = halo(rc, bc)

        @pl.when(ok)
        def _():
            copy.wait_send()

    loop(1, ndev, lambda i: gather(i).wait_send())
    loop(1, ncol, lambda i: reduce(i).wait_send())


def writer(fine_ref, coarse_ref, fine_out_ref, coarse_out_ref, sem):
    copies = [
        pltpu.make_async_copy(fine_ref, fine_out_ref, sem.at[0]),
        pltpu.make_async_copy(coarse_ref, coarse_out_ref, sem.at[1]),
    ]
    for copy in copies:
        copy.start()
    for copy in copies:
        copy.wait()


def body(
    image, noise_level, cond_table, ada_fine, fine_qkv, fine_scale, fine_out_w, fine_post,
    merge_w, coarse_in_w, ada_coarse, coarse_qkv, coarse_scale, coarse_out_w, coarse_post,
):
    nrow, ncol = lax.axis_size("row"), lax.axis_size("col")
    ndev = nrow * ncol
    rows, cols, width = image.shape
    tokens = rows * cols
    lw = coarse_qkv.shape[2]
    cw = coarse_in_w.shape[1]
    quarter = cw // 4
    side = TILE // (2 * POOL)
    smem = pl.BlockSpec(memory_space=pltpu.SMEM)
    vmem = pl.BlockSpec(memory_space=pltpu.VMEM)
    hbm = pl.BlockSpec(memory_space=pl.ANY)
    dma = pltpu.SemaphoreType.DMA
    fine, coarse = pl.pallas_call(
        functools.partial(kernel, nrow, ncol),
        out_shape=(
            jax.ShapeDtypeStruct((tokens, width), BF),
            jax.ShapeDtypeStruct((side, side, cw), BF),
        ),
        in_specs=[smem] * 3 + [hbm] * 12,
        out_specs=(hbm, vmem),
        scratch_shapes=[
            pltpu.VMEM((9, tokens, width), BF),
            pltpu.VMEM((2, tokens // QB, width, QB), BF),
            pltpu.VMEM((tokens, width), BF),
            pltpu.VMEM((2, ROWS, tokens), BF),
            pltpu.VMEM((2, tokens // QB, ROWS, QB), F32),
            pltpu.VMEM(cond_table.shape, F32),
            pltpu.VMEM(ada_fine.shape, F32),
            pltpu.VMEM(fine_qkv.shape, BF),
            pltpu.VMEM(fine_out_w.shape, BF),
            pltpu.VMEM((1, width), F32),
            pltpu.VMEM((1, cw), F32),
            pltpu.VMEM(merge_w.shape, BF),
            pltpu.VMEM(coarse_in_w.shape, BF),
            pltpu.VMEM(ada_coarse.shape, F32),
            pltpu.VMEM(coarse_qkv.shape, BF),
            pltpu.VMEM(coarse_out_w.shape, BF),
            pltpu.VMEM((tokens, width), BF),
            pltpu.VMEM((ndev, 16, quarter), BF),
            pltpu.VMEM((16, quarter), F32),
            pltpu.VMEM((ndev * 4, lw), F32),
            pltpu.VMEM((ncol, 16, quarter), BF),
            pltpu.VMEM((ncol, 16, quarter), BF),
            dma((13,)), dma((9,)), dma((9,)), dma((ndev,)), dma((ndev,)), dma((ncol,)), dma((ncol,)),
        ],
        compiler_params=pltpu.CompilerParams(
            collective_id=0, has_side_effects=True, vmem_limit_bytes=VMEM_BYTES
        ),
        cost_estimate=pl.CostEstimate(
            flops=tokens * tokens * 9 * width * 4, bytes_accessed=8 << 20,
            transcendentals=tokens * tokens * 18,
        ),
    )(
        noise_level, fine_scale, coarse_scale, image.reshape(tokens, width), cond_table, ada_fine,
        fine_qkv, fine_out_w, fine_post.reshape(1, -1), coarse_post.reshape(1, -1), merge_w,
        coarse_in_w, ada_coarse, coarse_qkv, coarse_out_w,
    )
    fine, coarse = pl.pallas_call(
        writer,
        out_shape=(
            jax.ShapeDtypeStruct(fine.shape, BF),
            jax.ShapeDtypeStruct(coarse.shape, BF),
        ),
        in_specs=[hbm, hbm],
        out_specs=(hbm, hbm),
        scratch_shapes=[dma((2,))],
        compiler_params=pltpu.CompilerParams(vmem_limit_bytes=VMEM_BYTES),
    )(fine, coarse)
    return fine.reshape(rows, cols, width), coarse


def solution(mesh):
    in_specs = (
        P(("noise", "row"), "col", None),
        P("noise"),
        P(),
        P(),
        P(),
        P(),
        P(),
        P(),
        P(),
        P(),
        P(),
        P(None, None, "col"),
        P("col"),
        P("col", None),
        P(),
    )
    out_specs = (P(("noise", "row"), "col", None), P(("noise", "row"), "col", None))
    return jax.shard_map(body, mesh=mesh, in_specs=in_specs, out_specs=out_specs, check_vma=False)
```

```python
import functools
import math

import jax
import jax.numpy as jnp
from jax import lax
from jax.experimental import pallas as pl
from jax.experimental.pallas import tpu as pltpu
from jax.sharding import PartitionSpec as P

HEAD = 64
TILE = 32
POOL = 8
QB = 512
VMEM_BYTES = 64 * 1024 * 1024 - 65536
EPS = 1e-6
MESH = pl.DeviceIdType.MESH
HIGHEST = lax.Precision.HIGHEST
BF = jnp.bfloat16
F32 = jnp.float32
SWAP = (0, 2, 1)


def mm(a, b):
    return jnp.dot(a, b, preferred_element_type=F32)


def iota(shape, dim):
    return lax.broadcasted_iota(jnp.int32, shape, dim)


def kernel(
    nrow, ncol, level_ref, fscale_ref, cscale_ref, image_hbm, table_hbm, adaf_hbm, fqkv_hbm,
    fout_hbm, fpost_hbm, cpost_hbm, merge_hbm, cin_hbm, adac_hbm, cqkv_hbm, cout_hbm,
    fine_hbm, coarse_ref,
    slots, qs, kt, vext, acc, acc_in, table_ref, ada_fine_ref, fqkv_ref, fout_ref, fpost_ref, cpost_ref,
    merge_w, cin_w, adac_w, cqkv_w, cout_w, fine_ref, gath, pack, qall,
    sbuf, rbuf, local_sem, hsend, hrecv, gsend, grecv, rsend, rrecv, asend, arecv,
):
    tokens, width = image_hbm.shape
    image_ref = slots.at[0]
    ndev = nrow * ncol
    row, col = lax.axis_index("row"), lax.axis_index("col")
    me = row * ncol + col
    sib = 1 - 2 * lax.rem(row, 2)

    loads = [
        pltpu.make_async_copy(src, dst, local_sem.at[i])
        for i, (src, dst) in enumerate(
            ((image_hbm, image_ref), (table_hbm, table_ref), (adaf_hbm, ada_fine_ref),
             (fqkv_hbm, fqkv_ref), (adac_hbm, adac_w), (fout_hbm, fout_ref),
             (fpost_hbm, fpost_ref), (cpost_hbm, cpost_ref), (merge_hbm, merge_w),
             (cin_hbm, cin_w), (cqkv_hbm, cqkv_w), (cout_hbm, cout_w))
        )
    ]
    for load in loads:
        load.start()

    barrier = pltpu.get_barrier_semaphore()

    def greet(i, carry):
        peer = lax.rem(me + i, ndev)
        pl.semaphore_signal(
            barrier, inc=1, device_id={"row": peer // ncol, "col": lax.rem(peer, ncol)},
            device_id_type=MESH,
        )
        return carry

    lax.fori_loop(1, ndev, greet, 0)
    for load in loads[:4]:
        load.wait()
    levels = table_ref.shape[0]
    hot = iota((levels, 1), 0) == level_ref[0]
    cond = jnp.sum(jnp.where(hot, table_ref[...], 0.0), axis=0, keepdims=True)
    cond = jnp.broadcast_to(cond, (8, cond.shape[1]))
    fine_gain = 1.0 + jnp.dot(cond, ada_fine_ref[...], precision=HIGHEST)[0:1]
    low = iota((1, width), 1) < HEAD
    same = (iota((width, width), 0) // HEAD) == (iota((width, width), 1) // HEAD)
    block_ones = jnp.where(same, 1.0, 0.0).astype(BF)

    all_ones = jnp.ones((width, width), BF)

    def normed(x):
        x = x.astype(F32)
        total = mm((x * x).astype(BF), all_ones)
        return (x * lax.rsqrt(total * (1.0 / width) + EPS) * fine_gain).astype(BF)

    def cosine(x):
        total = mm((x * x).astype(BF), block_ones)
        return x * lax.rsqrt(total * (1.0 / HEAD) + EPS)

    factor = math.log2(math.e) / HEAD
    qscale = jnp.where(low, fscale_ref[0] * factor, fscale_ref[1] * factor)

    def make_queries(owner, slot):
        queries = cosine(mm(normed(slots[slot]), fqkv_ref[:, 0:width])) * qscale
        qs[owner, 0] = jnp.where(low, queries, 0.0).astype(BF)
        qs[owner, 1] = jnp.where(low, 0.0, queries).astype(BF)

    make_queries(0, 0)
    acc[...] = jnp.zeros_like(acc)
    loads[4].wait()
    coarse_gain = 1.0 + jnp.dot(cond, adac_w[...], precision=HIGHEST)[0:1]

    pl.semaphore_wait(barrier, ndev - 1)

    def place(rc, bc):
        a = jnp.where(rc == 0, 0, jnp.where(rc == 1, sib, -sib))
        b = jnp.where(bc == 0, 0, jnp.where(bc == 1, -1, 1))
        r, c = row + a, col + b
        ok = (r >= 0) & (r < nrow) & (c >= 0) & (c < ncol)
        return r, c, ok

    def edge(r):
        return (r == 0) | (r == nrow - 1)

    shares = nrow > 2
    helper, helped = shares & edge(row), shares & edge(row + sib)
    blocks = tokens // QB

    def halo(rc, bc):
        r, c, ok = place(rc, bc)
        if (rc, bc) == (1, 2):
            ok = ok & jnp.logical_not(helper)
        there = SWAP[bc] * 3 + rc
        copy = pltpu.make_async_remote_copy(
            src_ref=image_ref, dst_ref=slots.at[there], send_sem=hsend.at[bc * 3 + rc],
            recv_sem=hrecv.at[there], device_id={"row": r, "col": c}, device_id_type=MESH,
        )
        return copy, ok

    order = [(1, 0), (2, 0), (0, 1), (0, 2), (1, 1), (1, 2), (2, 1), (2, 2)]
    for rc, bc in order:
        copy, ok = halo(rc, bc)

        @pl.when(ok)
        def _():
            copy.start()

    assist = pltpu.make_async_remote_copy(
        src_ref=acc.at[1], dst_ref=acc_in, send_sem=asend, recv_sem=arecv,
        device_id={"row": row + sib, "col": col}, device_id_type=MESH,
    )

    def step(s, carry):
        _, _, ok = place(lax.rem(s, 3), s // 3)
        ok = ok & jnp.logical_not(helped & (s == 4))

        @pl.when(ok)
        def _():
            @pl.when(s > 0)
            def _():
                pltpu.make_async_remote_copy(
                    src_ref=image_ref, dst_ref=slots.at[s], send_sem=hsend.at[s],
                    recv_sem=hrecv.at[s], device_id={"row": row, "col": col}, device_id_type=MESH,
                ).wait_recv()

            proj = mm(normed(slots[s]), fqkv_ref[:, width:])
            keys = cosine(proj[:, 0:width])
            kt[...] = keys.T.astype(BF)
            values = proj[:, width:]
            vext[0] = jnp.where(low, values, 1.0).astype(BF)
            vext[1] = jnp.where(low, 1.0, values).astype(BF)

            @pl.when(helper & (s == 1))
            def _():
                make_queries(1, 1)

            def blocks_of(owner):
                def block(i, c2):
                    rows = pl.ds(pl.multiple_of(i * QB, QB), QB)
                    s0 = mm(qs[owner, 0, rows, :], kt[...])
                    s1 = mm(qs[owner, 1, rows, :], kt[...])
                    p0 = jnp.exp2(s0).astype(BF)
                    acc[owner, 0, rows, :] += mm(p0, vext[0])
                    p1 = jnp.exp2(s1).astype(BF)
                    acc[owner, 1, rows, :] += mm(p1, vext[1])
                    return c2

                return block

            lax.fori_loop(jnp.where(helped & (s == 7), blocks // 2, 0), blocks, blocks_of(0), 0)
            if shares:
                extra = jnp.where(s == 3, blocks, jnp.where(s == 6, blocks // 2, 0))
                lax.fori_loop(0, jnp.where(helper, extra, 0), blocks_of(1), 0)

        if shares:
            @pl.when(helper & (s == 6))
            def _():
                assist.start()

        return carry

    lax.fori_loop(0, 9, step, 0)
    if shares:
        @pl.when(helped)
        def _():
            assist.wait_recv()
            acc[0] += acc_in[...]

    for load in loads[5:]:
        load.wait()

    a0, a1 = acc[0, 0], acc[0, 1]
    num = jnp.where(low, a0, a1)
    den = pltpu.roll(jnp.where(low, a1, a0), HEAD, 1)
    attended = (num / den).astype(BF)
    branch = mm(attended, fout_ref[...])
    branch = branch * lax.rsqrt(jnp.mean(branch * branch, axis=-1, keepdims=True) + EPS)
    fine = (slots[0].astype(F32) + branch * fpost_ref[...]).astype(BF)
    fine_ref[...] = fine
    store = pltpu.make_async_copy(fine_ref, fine_hbm, local_sem.at[len(loads)])
    store.start()
    at = iota((64, tokens), 1)
    r, c = at // TILE, at % TILE
    span = 2 * POOL
    target = ((r % 2) * 2 + c % 2) * 16 + (r // span) * (TILE // span) + c // span
    pick = jnp.where(iota((64, tokens), 0) == target, 1.0, 0.0).astype(BF)
    sums = mm(pick, fine) * (1.0 / (POOL * POOL))
    high = sums.astype(BF)
    rest = (sums - high.astype(F32)).astype(BF)
    pooled = jnp.zeros((16, merge_w.shape[1]), F32)
    for p in range(4):
        part_w = merge_w[p * width : (p + 1) * width, :]
        pooled = pooled + mm(high[p * 16 : p * 16 + 16], part_w) + mm(rest[p * 16 : p * 16 + 16], part_w)
    coarse_in = mm(pooled.astype(BF), cin_w[...])
    cn = coarse_in * lax.rsqrt(jnp.mean(coarse_in * coarse_in, axis=-1, keepdims=True) + EPS) * coarse_gain
    quarter = coarse_in.shape[1] // 4
    for j in range(4):
        pack[4 * j : 4 * j + 4, :] = cn[0:4, j * quarter : (j + 1) * quarter]
    gath[me] = pack[...].astype(BF)

    def gather(i):
        peer = lax.rem(me + i, ndev)
        return pltpu.make_async_remote_copy(
            src_ref=gath.at[me], dst_ref=gath.at[me], send_sem=gsend.at[i], recv_sem=grecv.at[me],
            device_id={"row": peer // ncol, "col": lax.rem(peer, ncol)}, device_id_type=MESH,
        )

    def gather_from(i):
        peer = lax.rem(me + i, ndev)
        return pltpu.make_async_remote_copy(
            src_ref=gath.at[peer], dst_ref=gath.at[peer], send_sem=gsend.at[i],
            recv_sem=grecv.at[peer],
            device_id={"row": peer // ncol, "col": lax.rem(peer, ncol)}, device_id_type=MESH,
        )

    def loop(low_at, high_at, do):
        def one(i, carry):
            do(i)
            return carry

        lax.fori_loop(low_at, high_at, one, 0)

    loop(1, ndev, lambda i: gather(i).start())
    loop(1, ndev, lambda i: gather_from(i).wait_recv())

    every = gath[...].reshape(ndev * 16, quarter)
    lw = cqkv_w.shape[2]
    count = ndev * 4
    out_at, in_at = iota((count, ndev * 16), 0), iota((count, ndev * 16), 1)
    proj = [jnp.zeros((count, lw), F32) for _ in range(3)]
    for j in range(4):
        wanted = (out_at // 4) * 16 + j * 4 + out_at % 4
        chosen = mm(jnp.where(in_at == wanted, 1.0, 0.0).astype(BF), every).astype(BF)
        for k in range(3):
            proj[k] = proj[k] + mm(chosen, cqkv_w[k, j * quarter : (j + 1) * quarter, :])
    head_same = (iota((lw, lw), 0) // HEAD) == (iota((lw, lw), 1) // HEAD)
    head_ones = jnp.where(head_same, 1.0, 0.0)

    def ccosine(x):
        total = jnp.dot(x * x, head_ones, precision=HIGHEST)
        return x * lax.rsqrt(total * (1.0 / HEAD) + EPS)

    qall[...] = ccosine(proj[0])
    keys = ccosine(proj[1]).astype(BF)
    values = proj[2].astype(BF)
    own = ncol * 4
    queries = qall[pl.ds(pl.multiple_of(row * own, own), own), :]
    heads = lw // HEAD
    lane_head = iota((own, lw), 1) // HEAD
    stack = jnp.concatenate(
        [jnp.where(lane_head == h, queries, 0.0) for h in range(heads)], axis=0
    ).astype(BF)
    scores = lax.dot_general(stack, keys, (((1,), (1,)), ((), ())), preferred_element_type=F32)
    results = jnp.zeros((own, lw), F32)
    for h in range(heads):
        expo = jnp.exp(scores[h * own : (h + 1) * own] * (cscale_ref[h] / HEAD))
        weights = (expo / jnp.sum(expo, axis=-1, keepdims=True)).astype(BF)
        results = results + jnp.where(lane_head == h, mm(weights, values), 0.0)
    partial = mm(results.astype(BF), cout_w[...])
    for k in range(ncol):
        for j in range(4):
            pack[4 * j : 4 * j + 4, :] = partial[4 * k : 4 * k + 4, j * quarter : (j + 1) * quarter]
        sbuf[k] = pack[...].astype(BF)
    rbuf[col] = sbuf[col]

    def reduce(i):
        peer = lax.rem(col + i, ncol)
        return pltpu.make_async_remote_copy(
            src_ref=sbuf.at[peer], dst_ref=rbuf.at[col], send_sem=rsend.at[i],
            recv_sem=rrecv.at[col], device_id={"row": row, "col": peer}, device_id_type=MESH,
        )

    def reduce_from(i):
        peer = lax.rem(col + i, ncol)
        return pltpu.make_async_remote_copy(
            src_ref=sbuf.at[peer], dst_ref=rbuf.at[peer], send_sem=rsend.at[i],
            recv_sem=rrecv.at[peer], device_id={"row": row, "col": peer}, device_id_type=MESH,
        )

    loop(1, ncol, lambda i: reduce(i).start())
    loop(1, ncol, lambda i: reduce_from(i).wait_recv())
    total = jnp.sum(rbuf[...].astype(F32), axis=0)
    pack[...] = total
    pieces = [pack[4 * j : 4 * j + 4, :] for j in range(4)]
    power = sum(jnp.sum(piece * piece, axis=-1, keepdims=True) for piece in pieces)
    inverse = lax.rsqrt(power * (1.0 / (4 * quarter)) + EPS)
    for j in range(4):
        at_j = slice(j * quarter, (j + 1) * quarter)
        y = coarse_in[0:4, at_j] + pieces[j] * inverse * cpost_ref[:, at_j]
        for k in range(coarse_ref.shape[0]):
            side = coarse_ref.shape[1]
            coarse_ref[k, :, at_j] = y[k * side : (k + 1) * side].astype(BF)

    store.wait()

    if shares:
        @pl.when(helper)
        def _():
            assist.wait_send()

    for rc, bc in order:
        copy, ok = halo(rc, bc)

        @pl.when(ok)
        def _():
            copy.wait_send()

    loop(1, ndev, lambda i: gather(i).wait_send())
    loop(1, ncol, lambda i: reduce(i).wait_send())


def body(
    image, noise_level, cond_table, ada_fine, fine_qkv, fine_scale, fine_out_w, fine_post,
    merge_w, coarse_in_w, ada_coarse, coarse_qkv, coarse_scale, coarse_out_w, coarse_post,
):
    nrow, ncol = lax.axis_size("row"), lax.axis_size("col")
    ndev = nrow * ncol
    rows, cols, width = image.shape
    tokens = rows * cols
    lw = coarse_qkv.shape[2]
    cw = coarse_in_w.shape[1]
    quarter = cw // 4
    side = TILE // (2 * POOL)
    smem = pl.BlockSpec(memory_space=pltpu.SMEM)
    vmem = pl.BlockSpec(memory_space=pltpu.VMEM)
    hbm = pl.BlockSpec(memory_space=pl.ANY)
    dma = pltpu.SemaphoreType.DMA
    fine, coarse = pl.pallas_call(
        functools.partial(kernel, nrow, ncol),
        out_shape=(
            jax.ShapeDtypeStruct((tokens, width), BF),
            jax.ShapeDtypeStruct((side, side, cw), BF),
        ),
        in_specs=[smem] * 3 + [hbm] * 12,
        out_specs=(hbm, vmem),
        scratch_shapes=[
            pltpu.VMEM((9, tokens, width), BF),
            pltpu.VMEM((2, 2, tokens, width), BF),
            pltpu.VMEM((width, tokens), BF),
            pltpu.VMEM((2, tokens, width), BF),
            pltpu.VMEM((2, 2, tokens, width), F32),
            pltpu.VMEM((2, tokens, width), F32),
            pltpu.VMEM(cond_table.shape, F32),
            pltpu.VMEM(ada_fine.shape, F32),
            pltpu.VMEM(fine_qkv.shape, BF),
            pltpu.VMEM(fine_out_w.shape, BF),
            pltpu.VMEM((1, width), F32),
            pltpu.VMEM((1, cw), F32),
            pltpu.VMEM(merge_w.shape, BF),
            pltpu.VMEM(coarse_in_w.shape, BF),
            pltpu.VMEM(ada_coarse.shape, F32),
            pltpu.VMEM(coarse_qkv.shape, BF),
            pltpu.VMEM(coarse_out_w.shape, BF),
            pltpu.VMEM((tokens, width), BF),
            pltpu.VMEM((ndev, 16, quarter), BF),
            pltpu.VMEM((16, quarter), F32),
            pltpu.VMEM((ndev * 4, lw), F32),
            pltpu.VMEM((ncol, 16, quarter), BF),
            pltpu.VMEM((ncol, 16, quarter), BF),
            dma((13,)), dma((9,)), dma((9,)), dma((ndev,)), dma((ndev,)), dma((ncol,)), dma((ncol,)),
            dma, dma,
        ],
        compiler_params=pltpu.CompilerParams(
            collective_id=0, has_side_effects=True, vmem_limit_bytes=VMEM_BYTES
        ),
        cost_estimate=pl.CostEstimate(
            flops=tokens * tokens * 9 * width * 4, bytes_accessed=8 << 20,
            transcendentals=tokens * tokens * 18,
        ),
    )(
        noise_level, fine_scale, coarse_scale, image.reshape(tokens, width), cond_table, ada_fine,
        fine_qkv, fine_out_w, fine_post.reshape(1, -1), coarse_post.reshape(1, -1), merge_w,
        coarse_in_w, ada_coarse, coarse_qkv, coarse_out_w,
    )
    return fine.reshape(rows, cols, width), coarse


def solution(mesh):
    in_specs = (
        P(("noise", "row"), "col", None),
        P("noise"),
        P(),
        P(),
        P(),
        P(),
        P(),
        P(),
        P(),
        P(),
        P(),
        P(None, None, "col"),
        P("col"),
        P("col", None),
        P(),
    )
    out_specs = (P(("noise", "row"), "col", None), P(("noise", "row"), "col", None))
    return jax.shard_map(body, mesh=mesh, in_specs=in_specs, out_specs=out_specs, check_vma=False)
```

```python
import functools
import math

import jax
import jax.numpy as jnp
from jax import lax
from jax.experimental import pallas as pl
from jax.experimental.pallas import tpu as pltpu
from jax.sharding import PartitionSpec as P

HEAD = 64
TILE = 32
POOL = 8
QB = 512
VMEM_BYTES = 64 * 1024 * 1024 - 65536
EPS = 1e-6
MESH = pl.DeviceIdType.MESH
HIGHEST = lax.Precision.HIGHEST
BF = jnp.bfloat16
F32 = jnp.float32
SWAP = (0, 2, 1)


def mm(a, b):
    return jnp.dot(a, b, preferred_element_type=F32)


def iota(shape, dim):
    return lax.broadcasted_iota(jnp.int32, shape, dim)


def kernel(
    nrow, ncol, level_ref, fscale_ref, cscale_ref, image_hbm, table_hbm, adaf_hbm, fqkv_hbm,
    fout_hbm, fpost_hbm, cpost_hbm, merge_hbm, cin_hbm, adac_hbm, cqkv_hbm, cout_hbm,
    fine_hbm, coarse_ref,
    slots, qs, kt, vext, acc, acc_in, table_ref, ada_fine_ref, fqkv_ref, fout_ref, fpost_ref, cpost_ref,
    merge_w, cin_w, adac_w, cqkv_w, cout_w, fine_ref, gath, pack, qall,
    sbuf, rbuf, local_sem, hsend, hrecv, gsend, grecv, rsend, rrecv, asend, arecv,
):
    tokens, width = image_hbm.shape
    image_ref = slots.at[0]
    ndev = nrow * ncol
    row, col = lax.axis_index("row"), lax.axis_index("col")
    me = row * ncol + col
    sib = 1 - 2 * lax.rem(row, 2)

    loads = [
        pltpu.make_async_copy(src, dst, local_sem.at[i])
        for i, (src, dst) in enumerate(
            ((image_hbm, image_ref), (table_hbm, table_ref), (adaf_hbm, ada_fine_ref),
             (fqkv_hbm, fqkv_ref), (adac_hbm, adac_w), (fout_hbm, fout_ref),
             (fpost_hbm, fpost_ref), (cpost_hbm, cpost_ref), (merge_hbm, merge_w),
             (cin_hbm, cin_w), (cqkv_hbm, cqkv_w), (cout_hbm, cout_w))
        )
    ]
    for load in loads:
        load.start()

    barrier = pltpu.get_barrier_semaphore()

    def greet(i, carry):
        peer = lax.rem(me + i, ndev)
        pl.semaphore_signal(
            barrier, inc=1, device_id={"row": peer // ncol, "col": lax.rem(peer, ncol)},
            device_id_type=MESH,
        )
        return carry

    lax.fori_loop(1, ndev, greet, 0)
    for load in loads[:4]:
        load.wait()
    levels = table_ref.shape[0]
    hot = iota((levels, 1), 0) == level_ref[0]
    cond = jnp.sum(jnp.where(hot, table_ref[...], 0.0), axis=0, keepdims=True)
    cond = jnp.broadcast_to(cond, (8, cond.shape[1]))
    fine_gain = 1.0 + jnp.dot(cond, ada_fine_ref[...], precision=HIGHEST)[0:1]
    low = iota((1, width), 1) < HEAD
    same = (iota((width, width), 0) // HEAD) == (iota((width, width), 1) // HEAD)
    block_ones = jnp.where(same, 1.0, 0.0).astype(BF)

    all_ones = jnp.ones((width, width), BF)

    def normed(x):
        x = x.astype(F32)
        total = mm((x * x).astype(BF), all_ones)
        return (x * lax.rsqrt(total * (1.0 / width) + EPS) * fine_gain).astype(BF)

    def cosine(x):
        total = mm((x * x).astype(BF), block_ones)
        return x * lax.rsqrt(total * (1.0 / HEAD) + EPS)

    factor = math.log2(math.e) / HEAD
    qscale = jnp.where(low, fscale_ref[0] * factor, fscale_ref[1] * factor)

    def make_queries(owner, slot):
        queries = cosine(mm(normed(slots[slot]), fqkv_ref[:, 0:width])) * qscale
        qs[owner, 0] = jnp.where(low, queries, 0.0).astype(BF)
        qs[owner, 1] = jnp.where(low, 0.0, queries).astype(BF)

    make_queries(0, 0)
    acc[...] = jnp.zeros_like(acc)
    loads[4].wait()
    coarse_gain = 1.0 + jnp.dot(cond, adac_w[...], precision=HIGHEST)[0:1]

    pl.semaphore_wait(barrier, ndev - 1)

    def place(rc, bc):
        a = jnp.where(rc == 0, 0, jnp.where(rc == 1, sib, -sib))
        b = jnp.where(bc == 0, 0, jnp.where(bc == 1, -1, 1))
        r, c = row + a, col + b
        ok = (r >= 0) & (r < nrow) & (c >= 0) & (c < ncol)
        return r, c, ok

    def edge(r):
        return (r == 0) | (r == nrow - 1)

    shares = nrow > 2
    helper, helped = shares & edge(row), shares & edge(row + sib)
    blocks = tokens // QB

    def halo(rc, bc):
        r, c, ok = place(rc, bc)
        if (rc, bc) == (1, 2):
            ok = ok & jnp.logical_not(helper)
        there = SWAP[bc] * 3 + rc
        copy = pltpu.make_async_remote_copy(
            src_ref=image_ref, dst_ref=slots.at[there], send_sem=hsend.at[bc * 3 + rc],
            recv_sem=hrecv.at[there], device_id={"row": r, "col": c}, device_id_type=MESH,
        )
        return copy, ok

    order = [(1, 0), (2, 0), (0, 1), (0, 2), (1, 1), (1, 2), (2, 1), (2, 2)]
    for rc, bc in order:
        copy, ok = halo(rc, bc)

        @pl.when(ok)
        def _():
            copy.start()

    assist = pltpu.make_async_remote_copy(
        src_ref=acc.at[1], dst_ref=acc_in, send_sem=asend, recv_sem=arecv,
        device_id={"row": row + sib, "col": col}, device_id_type=MESH,
    )

    def step(s, carry):
        _, _, ok = place(lax.rem(s, 3), s // 3)
        ok = ok & jnp.logical_not(helped & (s == 4))

        @pl.when(ok)
        def _():
            @pl.when(s > 0)
            def _():
                pltpu.make_async_remote_copy(
                    src_ref=image_ref, dst_ref=slots.at[s], send_sem=hsend.at[s],
                    recv_sem=hrecv.at[s], device_id={"row": row, "col": col}, device_id_type=MESH,
                ).wait_recv()

            proj = mm(normed(slots[s]), fqkv_ref[:, width:])
            keys = cosine(proj[:, 0:width])
            kt[...] = keys.T.astype(BF)
            values = proj[:, width:]
            vext[0] = jnp.where(low, values, 1.0).astype(BF)
            vext[1] = jnp.where(low, 1.0, values).astype(BF)

            @pl.when(helper & (s == 1))
            def _():
                make_queries(1, 1)

            def blocks_of(owner):
                def block(i, c2):
                    rows = pl.ds(pl.multiple_of(i * QB, QB), QB)
                    s0 = mm(qs[owner, 0, rows, :], kt[...])
                    s1 = mm(qs[owner, 1, rows, :], kt[...])
                    p0 = jnp.exp2(s0.astype(BF))
                    acc[owner, 0, rows, :] += mm(p0, vext[0])
                    p1 = jnp.exp2(s1.astype(BF))
                    acc[owner, 1, rows, :] += mm(p1, vext[1])
                    return c2

                return block

            lax.fori_loop(jnp.where(helped & (s == 7), blocks // 2, 0), blocks, blocks_of(0), 0)
            if shares:
                extra = jnp.where(s == 3, blocks, jnp.where(s == 6, blocks // 2, 0))
                lax.fori_loop(0, jnp.where(helper, extra, 0), blocks_of(1), 0)

        if shares:
            @pl.when(helper & (s == 6))
            def _():
                assist.start()

        return carry

    lax.fori_loop(0, 9, step, 0)
    if shares:
        @pl.when(helped)
        def _():
            assist.wait_recv()
            acc[0] += acc_in[...]

    for load in loads[5:]:
        load.wait()

    a0, a1 = acc[0, 0], acc[0, 1]
    num = jnp.where(low, a0, a1)
    den = pltpu.roll(jnp.where(low, a1, a0), HEAD, 1)
    attended = (num / den).astype(BF)
    branch = mm(attended, fout_ref[...])
    branch = branch * lax.rsqrt(jnp.mean(branch * branch, axis=-1, keepdims=True) + EPS)
    fine = (slots[0].astype(F32) + branch * fpost_ref[...]).astype(BF)
    fine_ref[...] = fine
    store = pltpu.make_async_copy(fine_ref, fine_hbm, local_sem.at[len(loads)])
    store.start()
    at = iota((64, tokens), 1)
    r, c = at // TILE, at % TILE
    span = 2 * POOL
    target = ((r % 2) * 2 + c % 2) * 16 + (r // span) * (TILE // span) + c // span
    pick = jnp.where(iota((64, tokens), 0) == target, 1.0, 0.0).astype(BF)
    sums = mm(pick, fine) * (1.0 / (POOL * POOL))
    high = sums.astype(BF)
    rest = (sums - high.astype(F32)).astype(BF)
    pooled = jnp.zeros((16, merge_w.shape[1]), F32)
    for p in range(4):
        part_w = merge_w[p * width : (p + 1) * width, :]
        pooled = pooled + mm(high[p * 16 : p * 16 + 16], part_w) + mm(rest[p * 16 : p * 16 + 16], part_w)
    coarse_in = mm(pooled.astype(BF), cin_w[...])
    cn = coarse_in * lax.rsqrt(jnp.mean(coarse_in * coarse_in, axis=-1, keepdims=True) + EPS) * coarse_gain
    quarter = coarse_in.shape[1] // 4
    for j in range(4):
        pack[4 * j : 4 * j + 4, :] = cn[0:4, j * quarter : (j + 1) * quarter]
    gath[me] = pack[...].astype(BF)

    def gather(i):
        peer = lax.rem(me + i, ndev)
        return pltpu.make_async_remote_copy(
            src_ref=gath.at[me], dst_ref=gath.at[me], send_sem=gsend.at[i], recv_sem=grecv.at[me],
            device_id={"row": peer // ncol, "col": lax.rem(peer, ncol)}, device_id_type=MESH,
        )

    def gather_from(i):
        peer = lax.rem(me + i, ndev)
        return pltpu.make_async_remote_copy(
            src_ref=gath.at[peer], dst_ref=gath.at[peer], send_sem=gsend.at[i],
            recv_sem=grecv.at[peer],
            device_id={"row": peer // ncol, "col": lax.rem(peer, ncol)}, device_id_type=MESH,
        )

    def loop(low_at, high_at, do):
        def one(i, carry):
            do(i)
            return carry

        lax.fori_loop(low_at, high_at, one, 0)

    loop(1, ndev, lambda i: gather(i).start())
    loop(1, ndev, lambda i: gather_from(i).wait_recv())

    every = gath[...].reshape(ndev * 16, quarter)
    lw = cqkv_w.shape[2]
    count = ndev * 4
    out_at, in_at = iota((count, ndev * 16), 0), iota((count, ndev * 16), 1)
    proj = [jnp.zeros((count, lw), F32) for _ in range(3)]
    for j in range(4):
        wanted = (out_at // 4) * 16 + j * 4 + out_at % 4
        chosen = mm(jnp.where(in_at == wanted, 1.0, 0.0).astype(BF), every).astype(BF)
        for k in range(3):
            proj[k] = proj[k] + mm(chosen, cqkv_w[k, j * quarter : (j + 1) * quarter, :])
    head_same = (iota((lw, lw), 0) // HEAD) == (iota((lw, lw), 1) // HEAD)
    head_ones = jnp.where(head_same, 1.0, 0.0)

    def ccosine(x):
        total = jnp.dot(x * x, head_ones, precision=HIGHEST)
        return x * lax.rsqrt(total * (1.0 / HEAD) + EPS)

    qall[...] = ccosine(proj[0])
    keys = ccosine(proj[1]).astype(BF)
    values = proj[2].astype(BF)
    own = ncol * 4
    queries = qall[pl.ds(pl.multiple_of(row * own, own), own), :]
    heads = lw // HEAD
    lane_head = iota((own, lw), 1) // HEAD
    stack = jnp.concatenate(
        [jnp.where(lane_head == h, queries, 0.0) for h in range(heads)], axis=0
    ).astype(BF)
    scores = lax.dot_general(stack, keys, (((1,), (1,)), ((), ())), preferred_element_type=F32)
    results = jnp.zeros((own, lw), F32)
    for h in range(heads):
        expo = jnp.exp(scores[h * own : (h + 1) * own] * (cscale_ref[h] / HEAD))
        weights = (expo / jnp.sum(expo, axis=-1, keepdims=True)).astype(BF)
        results = results + jnp.where(lane_head == h, mm(weights, values), 0.0)
    partial = mm(results.astype(BF), cout_w[...])
    for k in range(ncol):
        for j in range(4):
            pack[4 * j : 4 * j + 4, :] = partial[4 * k : 4 * k + 4, j * quarter : (j + 1) * quarter]
        sbuf[k] = pack[...].astype(BF)
    rbuf[col] = sbuf[col]

    def reduce(i):
        peer = lax.rem(col + i, ncol)
        return pltpu.make_async_remote_copy(
            src_ref=sbuf.at[peer], dst_ref=rbuf.at[col], send_sem=rsend.at[i],
            recv_sem=rrecv.at[col], device_id={"row": row, "col": peer}, device_id_type=MESH,
        )

    def reduce_from(i):
        peer = lax.rem(col + i, ncol)
        return pltpu.make_async_remote_copy(
            src_ref=sbuf.at[peer], dst_ref=rbuf.at[peer], send_sem=rsend.at[i],
            recv_sem=rrecv.at[peer], device_id={"row": row, "col": peer}, device_id_type=MESH,
        )

    loop(1, ncol, lambda i: reduce(i).start())
    loop(1, ncol, lambda i: reduce_from(i).wait_recv())
    total = jnp.sum(rbuf[...].astype(F32), axis=0)
    pack[...] = total
    pieces = [pack[4 * j : 4 * j + 4, :] for j in range(4)]
    power = sum(jnp.sum(piece * piece, axis=-1, keepdims=True) for piece in pieces)
    inverse = lax.rsqrt(power * (1.0 / (4 * quarter)) + EPS)
    for j in range(4):
        at_j = slice(j * quarter, (j + 1) * quarter)
        y = coarse_in[0:4, at_j] + pieces[j] * inverse * cpost_ref[:, at_j]
        for k in range(coarse_ref.shape[0]):
            side = coarse_ref.shape[1]
            coarse_ref[k, :, at_j] = y[k * side : (k + 1) * side].astype(BF)

    store.wait()

    if shares:
        @pl.when(helper)
        def _():
            assist.wait_send()

    for rc, bc in order:
        copy, ok = halo(rc, bc)

        @pl.when(ok)
        def _():
            copy.wait_send()

    loop(1, ndev, lambda i: gather(i).wait_send())
    loop(1, ncol, lambda i: reduce(i).wait_send())


def body(
    image, noise_level, cond_table, ada_fine, fine_qkv, fine_scale, fine_out_w, fine_post,
    merge_w, coarse_in_w, ada_coarse, coarse_qkv, coarse_scale, coarse_out_w, coarse_post,
):
    nrow, ncol = lax.axis_size("row"), lax.axis_size("col")
    ndev = nrow * ncol
    rows, cols, width = image.shape
    tokens = rows * cols
    lw = coarse_qkv.shape[2]
    cw = coarse_in_w.shape[1]
    quarter = cw // 4
    side = TILE // (2 * POOL)
    smem = pl.BlockSpec(memory_space=pltpu.SMEM)
    vmem = pl.BlockSpec(memory_space=pltpu.VMEM)
    hbm = pl.BlockSpec(memory_space=pl.ANY)
    dma = pltpu.SemaphoreType.DMA
    fine, coarse = pl.pallas_call(
        functools.partial(kernel, nrow, ncol),
        out_shape=(
            jax.ShapeDtypeStruct((tokens, width), BF),
            jax.ShapeDtypeStruct((side, side, cw), BF),
        ),
        in_specs=[smem] * 3 + [hbm] * 12,
        out_specs=(hbm, vmem),
        scratch_shapes=[
            pltpu.VMEM((9, tokens, width), BF),
            pltpu.VMEM((2, 2, tokens, width), BF),
            pltpu.VMEM((width, tokens), BF),
            pltpu.VMEM((2, tokens, width), BF),
            pltpu.VMEM((2, 2, tokens, width), F32),
            pltpu.VMEM((2, tokens, width), F32),
            pltpu.VMEM(cond_table.shape, F32),
            pltpu.VMEM(ada_fine.shape, F32),
            pltpu.VMEM(fine_qkv.shape, BF),
            pltpu.VMEM(fine_out_w.shape, BF),
            pltpu.VMEM((1, width), F32),
            pltpu.VMEM((1, cw), F32),
            pltpu.VMEM(merge_w.shape, BF),
            pltpu.VMEM(coarse_in_w.shape, BF),
            pltpu.VMEM(ada_coarse.shape, F32),
            pltpu.VMEM(coarse_qkv.shape, BF),
            pltpu.VMEM(coarse_out_w.shape, BF),
            pltpu.VMEM((tokens, width), BF),
            pltpu.VMEM((ndev, 16, quarter), BF),
            pltpu.VMEM((16, quarter), F32),
            pltpu.VMEM((ndev * 4, lw), F32),
            pltpu.VMEM((ncol, 16, quarter), BF),
            pltpu.VMEM((ncol, 16, quarter), BF),
            dma((13,)), dma((9,)), dma((9,)), dma((ndev,)), dma((ndev,)), dma((ncol,)), dma((ncol,)),
            dma, dma,
        ],
        compiler_params=pltpu.CompilerParams(
            collective_id=0, has_side_effects=True, vmem_limit_bytes=VMEM_BYTES
        ),
        cost_estimate=pl.CostEstimate(
            flops=tokens * tokens * 9 * width * 4, bytes_accessed=8 << 20,
            transcendentals=tokens * tokens * 18,
        ),
    )(
        noise_level, fine_scale, coarse_scale, image.reshape(tokens, width), cond_table, ada_fine,
        fine_qkv, fine_out_w, fine_post.reshape(1, -1), coarse_post.reshape(1, -1), merge_w,
        coarse_in_w, ada_coarse, coarse_qkv, coarse_out_w,
    )
    return fine.reshape(rows, cols, width), coarse


def solution(mesh):
    in_specs = (
        P(("noise", "row"), "col", None),
        P("noise"),
        P(),
        P(),
        P(),
        P(),
        P(),
        P(),
        P(),
        P(),
        P(),
        P(None, None, "col"),
        P("col"),
        P("col", None),
        P(),
    )
    out_specs = (P(("noise", "row"), "col", None), P(("noise", "row"), "col", None))
    return jax.shard_map(body, mesh=mesh, in_specs=in_specs, out_specs=out_specs, check_vma=False)
```

```python
import functools
import math

import jax
import jax.numpy as jnp
from jax import lax
from jax.experimental import pallas as pl
from jax.experimental.pallas import tpu as pltpu
from jax.sharding import PartitionSpec as P

HEAD = 64
TILE = 32
POOL = 8
QB = 512
VMEM_BYTES = 64 * 1024 * 1024 - 65536
EPS = 1e-6
MESH = pl.DeviceIdType.MESH
BF = jnp.bfloat16
F32 = jnp.float32
SWAP = (0, 2, 1)


def mm(a, b):
    return jnp.dot(a, b, preferred_element_type=F32)


def iota(shape, dim):
    return lax.broadcasted_iota(jnp.int32, shape, dim)


def kernel(
    nrow, ncol, level_ref, fscale_ref, cscale_ref, image_hbm, table_hbm, adaf_hbm, fqkv_hbm,
    fout_hbm, fpost_hbm, cpost_hbm, merge_hbm, cin_hbm, adac_hbm, cqkv_hbm, cout_hbm,
    fine_hbm, coarse_ref,
    slots, qs, kt, vext, acc, acc_in, table_ref, ada_fine_ref, fqkv_ref, fout_ref, fpost_ref, cpost_ref,
    merge_w, cin_w, adac_w, cqkv_w, cout_w, fine_ref, gath, pack, qall,
    sbuf, rbuf, local_sem, hsend, hrecv, gsend, grecv, rsend, rrecv, asend, arecv,
):
    tokens, width = image_hbm.shape
    image_ref = slots.at[0]
    ndev = nrow * ncol
    row, col = lax.axis_index("row"), lax.axis_index("col")
    me = row * ncol + col
    sib = 1 - 2 * lax.rem(row, 2)

    loads = [
        pltpu.make_async_copy(src, dst, local_sem.at[i])
        for i, (src, dst) in enumerate(
            ((image_hbm, image_ref), (table_hbm, table_ref), (adaf_hbm, ada_fine_ref),
             (fqkv_hbm, fqkv_ref), (adac_hbm, adac_w), (fout_hbm, fout_ref),
             (fpost_hbm, fpost_ref), (cpost_hbm, cpost_ref), (merge_hbm, merge_w),
             (cin_hbm, cin_w), (cqkv_hbm, cqkv_w), (cout_hbm, cout_w))
        )
    ]
    for load in loads:
        load.start()

    barrier = pltpu.get_barrier_semaphore()

    def greet(i, carry):
        peer = lax.rem(me + i, ndev)
        pl.semaphore_signal(
            barrier, inc=1, device_id={"row": peer // ncol, "col": lax.rem(peer, ncol)},
            device_id_type=MESH,
        )
        return carry

    lax.fori_loop(1, ndev, greet, 0)
    for load in loads[:4]:
        load.wait()
    levels = table_ref.shape[0]
    hot = iota((levels, 1), 0) == level_ref[0]
    cond = jnp.sum(jnp.where(hot, table_ref[...], 0.0), axis=0, keepdims=True)
    cond = jnp.broadcast_to(cond, (8, cond.shape[1])).T[:, 0:1]
    fine_gain = 1.0 + jnp.sum(cond * ada_fine_ref[...], axis=0, keepdims=True)
    low = iota((1, width), 1) < HEAD
    same = (iota((width, width), 0) // HEAD) == (iota((width, width), 1) // HEAD)
    block_ones = jnp.where(same, 1.0, 0.0).astype(BF)

    all_ones = jnp.ones((width, width), BF)

    def normed(x):
        x = x.astype(F32)
        total = mm((x * x).astype(BF), all_ones)
        return (x * lax.rsqrt(total * (1.0 / width) + EPS) * fine_gain).astype(BF)

    def cosine(x):
        total = mm((x * x).astype(BF), block_ones)
        return x * lax.rsqrt(total * (1.0 / HEAD) + EPS)

    factor = math.log2(math.e) / HEAD
    qscale = jnp.where(low, fscale_ref[0] * factor, fscale_ref[1] * factor)

    def make_queries(owner, slot):
        queries = cosine(mm(normed(slots[slot]), fqkv_ref[:, 0:width])) * qscale
        qs[owner, 0] = jnp.where(low, queries, 0.0).astype(BF)
        qs[owner, 1] = jnp.where(low, 0.0, queries).astype(BF)

    make_queries(0, 0)
    acc[...] = jnp.zeros_like(acc)
    loads[4].wait()
    coarse_gain = 1.0 + jnp.sum(cond * adac_w[...], axis=0, keepdims=True)

    pl.semaphore_wait(barrier, ndev - 1)

    def place(rc, bc):
        a = jnp.where(rc == 0, 0, jnp.where(rc == 1, sib, -sib))
        b = jnp.where(bc == 0, 0, jnp.where(bc == 1, -1, 1))
        r, c = row + a, col + b
        ok = (r >= 0) & (r < nrow) & (c >= 0) & (c < ncol)
        return r, c, ok

    def edge(r):
        return (r == 0) | (r == nrow - 1)

    shares = nrow > 2
    helper, helped = shares & edge(row), shares & edge(row + sib)
    blocks = tokens // QB

    def halo(rc, bc):
        r, c, ok = place(rc, bc)
        if (rc, bc) == (1, 2):
            ok = ok & jnp.logical_not(helper)
        there = SWAP[bc] * 3 + rc
        copy = pltpu.make_async_remote_copy(
            src_ref=image_ref, dst_ref=slots.at[there], send_sem=hsend.at[bc * 3 + rc],
            recv_sem=hrecv.at[there], device_id={"row": r, "col": c}, device_id_type=MESH,
        )
        return copy, ok

    order = [(1, 0), (2, 0), (0, 1), (0, 2), (1, 1), (1, 2), (2, 1), (2, 2)]
    for rc, bc in order:
        copy, ok = halo(rc, bc)

        @pl.when(ok)
        def _():
            copy.start()

    assist = pltpu.make_async_remote_copy(
        src_ref=acc.at[1], dst_ref=acc_in, send_sem=asend, recv_sem=arecv,
        device_id={"row": row + sib, "col": col}, device_id_type=MESH,
    )

    def step(s, carry):
        _, _, ok = place(lax.rem(s, 3), s // 3)
        ok = ok & jnp.logical_not(helped & (s == 4))

        @pl.when(ok)
        def _():
            @pl.when(s > 0)
            def _():
                pltpu.make_async_remote_copy(
                    src_ref=image_ref, dst_ref=slots.at[s], send_sem=hsend.at[s],
                    recv_sem=hrecv.at[s], device_id={"row": row, "col": col}, device_id_type=MESH,
                ).wait_recv()

            proj = mm(normed(slots[s]), fqkv_ref[:, width:])
            keys = cosine(proj[:, 0:width])
            kt[...] = keys.T.astype(BF)
            values = proj[:, width:]
            vext[0] = jnp.where(low, values, 1.0).astype(BF)
            vext[1] = jnp.where(low, 1.0, values).astype(BF)

            @pl.when(helper & (s == 1))
            def _():
                make_queries(1, 1)

            def blocks_of(owner):
                def block(i, c2):
                    rows = pl.ds(pl.multiple_of(i * QB, QB), QB)
                    s0 = mm(qs[owner, 0, rows, :], kt[...])
                    s1 = mm(qs[owner, 1, rows, :], kt[...])
                    p0 = jnp.exp2(s0).astype(BF)
                    acc[owner, 0, rows, :] += mm(p0, vext[0])
                    p1 = jnp.exp2(s1).astype(BF)
                    acc[owner, 1, rows, :] += mm(p1, vext[1])
                    return c2

                return block

            lax.fori_loop(jnp.where(helped & (s == 7), blocks // 2, 0), blocks, blocks_of(0), 0)
            if shares:
                extra = jnp.where(s == 3, blocks, jnp.where(s == 6, blocks // 2, 0))
                lax.fori_loop(0, jnp.where(helper, extra, 0), blocks_of(1), 0)

        if shares:
            @pl.when(helper & (s == 6))
            def _():
                assist.start()

        return carry

    lax.fori_loop(0, 9, step, 0)
    if shares:
        @pl.when(helped)
        def _():
            assist.wait_recv()
            acc[0] += acc_in[...]

    for load in loads[5:]:
        load.wait()

    a0, a1 = acc[0, 0], acc[0, 1]
    num = jnp.where(low, a0, a1)
    den = pltpu.roll(jnp.where(low, a1, a0), HEAD, 1)
    attended = (num / den).astype(BF)
    branch = mm(attended, fout_ref[...])
    branch = branch * lax.rsqrt(jnp.mean(branch * branch, axis=-1, keepdims=True) + EPS)
    fine = (slots[0].astype(F32) + branch * fpost_ref[...]).astype(BF)
    fine_ref[...] = fine
    store = pltpu.make_async_copy(fine_ref, fine_hbm, local_sem.at[len(loads)])
    store.start()
    at = iota((64, tokens), 1)
    r, c = at // TILE, at % TILE
    span = 2 * POOL
    target = ((r % 2) * 2 + c % 2) * 16 + (r // span) * (TILE // span) + c // span
    pick = jnp.where(iota((64, tokens), 0) == target, 1.0, 0.0).astype(BF)
    sums = mm(pick, fine) * (1.0 / (POOL * POOL))
    high = sums.astype(BF)
    rest = (sums - high.astype(F32)).astype(BF)
    both = jnp.concatenate(
        [
            jnp.concatenate([x[p * 16 : p * 16 + 16] for p in range(4)], axis=1)
            for x in (high, rest)
        ],
        axis=0,
    )
    pooled = mm(both, merge_w[...])
    pooled = pooled[0:16] + pooled[16:32]
    coarse_in = mm(pooled.astype(BF), cin_w[...])
    cn = coarse_in * lax.rsqrt(jnp.mean(coarse_in * coarse_in, axis=-1, keepdims=True) + EPS) * coarse_gain
    quarter = coarse_in.shape[1] // 4
    for j in range(4):
        pack[4 * j : 4 * j + 4, :] = cn[0:4, j * quarter : (j + 1) * quarter]
    gath[me] = pack[...].astype(BF)

    def gather(i):
        peer = lax.rem(me + i, ndev)
        return pltpu.make_async_remote_copy(
            src_ref=gath.at[me], dst_ref=gath.at[me], send_sem=gsend.at[i], recv_sem=grecv.at[me],
            device_id={"row": peer // ncol, "col": lax.rem(peer, ncol)}, device_id_type=MESH,
        )

    def gather_from(i):
        peer = lax.rem(me + i, ndev)
        return pltpu.make_async_remote_copy(
            src_ref=gath.at[peer], dst_ref=gath.at[peer], send_sem=gsend.at[i],
            recv_sem=grecv.at[peer],
            device_id={"row": peer // ncol, "col": lax.rem(peer, ncol)}, device_id_type=MESH,
        )

    def loop(low_at, high_at, do):
        def one(i, carry):
            do(i)
            return carry

        lax.fori_loop(low_at, high_at, one, 0)

    loop(1, ndev, lambda i: gather(i).start())
    loop(1, ndev, lambda i: gather_from(i).wait_recv())

    every = gath[...].reshape(ndev * 16, quarter)
    lw = cqkv_w.shape[2]
    count = ndev * 4
    out_at, in_at = iota((count, ndev * 16), 0), iota((count, ndev * 16), 1)
    chosen = []
    for j in range(4):
        wanted = (out_at // 4) * 16 + j * 4 + out_at % 4
        pick = jnp.where(in_at == wanted, 1.0, 0.0).astype(BF)
        chosen.append(mm(pick, every).astype(BF))
    chosen = jnp.concatenate(chosen, axis=1)
    proj = [mm(chosen, cqkv_w[k]) for k in range(3)]
    head_same = (iota((lw, lw), 0) // HEAD) == (iota((lw, lw), 1) // HEAD)
    head_ones = jnp.where(head_same, 1.0, 0.0).astype(BF)
    pair = jnp.concatenate(proj[0:2], axis=0)
    pair = pair * lax.rsqrt(mm((pair * pair).astype(BF), head_ones) * (1.0 / HEAD) + EPS)
    qall[...] = pair[0:count]
    keys = pair[count:].astype(BF)
    values = proj[2].astype(BF)
    own = ncol * 4
    queries = qall[pl.ds(pl.multiple_of(row * own, own), own), :]
    heads = lw // HEAD
    lane_head = iota((own, lw), 1) // HEAD
    stack = jnp.concatenate(
        [jnp.where(lane_head == h, queries, 0.0) for h in range(heads)], axis=0
    ).astype(BF)
    scores = lax.dot_general(stack, keys, (((1,), (1,)), ((), ())), preferred_element_type=F32)
    row_head = iota((heads * own, 1), 0) // own
    factors = jnp.zeros((heads * own, 1), F32)
    for h in range(heads):
        factors = jnp.where(row_head == h, cscale_ref[h] / HEAD, factors)
    expo = jnp.exp(scores * factors)
    weights = (expo / jnp.sum(expo, axis=-1, keepdims=True)).astype(BF)
    mixed = jnp.where(iota((heads * own, lw), 1) // HEAD == row_head, mm(weights, values), 0.0)
    results = sum(mixed[h * own : (h + 1) * own] for h in range(heads))
    partial = mm(results.astype(BF), cout_w[...])
    for k in range(ncol):
        for j in range(4):
            pack[4 * j : 4 * j + 4, :] = partial[4 * k : 4 * k + 4, j * quarter : (j + 1) * quarter]
        sbuf[k] = pack[...].astype(BF)
    rbuf[col] = sbuf[col]

    def reduce(i):
        peer = lax.rem(col + i, ncol)
        return pltpu.make_async_remote_copy(
            src_ref=sbuf.at[peer], dst_ref=rbuf.at[col], send_sem=rsend.at[i],
            recv_sem=rrecv.at[col], device_id={"row": row, "col": peer}, device_id_type=MESH,
        )

    def reduce_from(i):
        peer = lax.rem(col + i, ncol)
        return pltpu.make_async_remote_copy(
            src_ref=sbuf.at[peer], dst_ref=rbuf.at[peer], send_sem=rsend.at[i],
            recv_sem=rrecv.at[peer], device_id={"row": row, "col": peer}, device_id_type=MESH,
        )

    loop(1, ncol, lambda i: reduce(i).start())
    loop(1, ncol, lambda i: reduce_from(i).wait_recv())
    total = jnp.sum(rbuf[...].astype(F32), axis=0)
    pack[...] = total
    pieces = [pack[4 * j : 4 * j + 4, :] for j in range(4)]
    power = sum(jnp.sum(piece * piece, axis=-1, keepdims=True) for piece in pieces)
    inverse = lax.rsqrt(power * (1.0 / (4 * quarter)) + EPS)
    for j in range(4):
        at_j = slice(j * quarter, (j + 1) * quarter)
        y = coarse_in[0:4, at_j] + pieces[j] * inverse * cpost_ref[:, at_j]
        for k in range(coarse_ref.shape[0]):
            side = coarse_ref.shape[1]
            coarse_ref[k, :, at_j] = y[k * side : (k + 1) * side].astype(BF)

    store.wait()

    if shares:
        @pl.when(helper)
        def _():
            assist.wait_send()

    for rc, bc in order:
        copy, ok = halo(rc, bc)

        @pl.when(ok)
        def _():
            copy.wait_send()

    loop(1, ndev, lambda i: gather(i).wait_send())
    loop(1, ncol, lambda i: reduce(i).wait_send())


def body(
    image, noise_level, cond_table, ada_fine, fine_qkv, fine_scale, fine_out_w, fine_post,
    merge_w, coarse_in_w, ada_coarse, coarse_qkv, coarse_scale, coarse_out_w, coarse_post,
):
    nrow, ncol = lax.axis_size("row"), lax.axis_size("col")
    ndev = nrow * ncol
    rows, cols, width = image.shape
    tokens = rows * cols
    lw = coarse_qkv.shape[2]
    cw = coarse_in_w.shape[1]
    quarter = cw // 4
    side = TILE // (2 * POOL)
    smem = pl.BlockSpec(memory_space=pltpu.SMEM)
    vmem = pl.BlockSpec(memory_space=pltpu.VMEM)
    hbm = pl.BlockSpec(memory_space=pl.ANY)
    dma = pltpu.SemaphoreType.DMA
    fine, coarse = pl.pallas_call(
        functools.partial(kernel, nrow, ncol),
        out_shape=(
            jax.ShapeDtypeStruct((tokens, width), BF),
            jax.ShapeDtypeStruct((side, side, cw), BF),
        ),
        in_specs=[smem] * 3 + [hbm] * 12,
        out_specs=(hbm, vmem),
        scratch_shapes=[
            pltpu.VMEM((9, tokens, width), BF),
            pltpu.VMEM((2, 2, tokens, width), BF),
            pltpu.VMEM((width, tokens), BF),
            pltpu.VMEM((2, tokens, width), BF),
            pltpu.VMEM((2, 2, tokens, width), F32),
            pltpu.VMEM((2, tokens, width), F32),
            pltpu.VMEM(cond_table.shape, F32),
            pltpu.VMEM(ada_fine.shape, F32),
            pltpu.VMEM(fine_qkv.shape, BF),
            pltpu.VMEM(fine_out_w.shape, BF),
            pltpu.VMEM((1, width), F32),
            pltpu.VMEM((1, cw), F32),
            pltpu.VMEM(merge_w.shape, BF),
            pltpu.VMEM(coarse_in_w.shape, BF),
            pltpu.VMEM(ada_coarse.shape, F32),
            pltpu.VMEM(coarse_qkv.shape, BF),
            pltpu.VMEM(coarse_out_w.shape, BF),
            pltpu.VMEM((tokens, width), BF),
            pltpu.VMEM((ndev, 16, quarter), BF),
            pltpu.VMEM((16, quarter), F32),
            pltpu.VMEM((ndev * 4, lw), F32),
            pltpu.VMEM((ncol, 16, quarter), BF),
            pltpu.VMEM((ncol, 16, quarter), BF),
            dma((13,)), dma((9,)), dma((9,)), dma((ndev,)), dma((ndev,)), dma((ncol,)), dma((ncol,)),
            dma, dma,
        ],
        compiler_params=pltpu.CompilerParams(
            collective_id=0, has_side_effects=True, vmem_limit_bytes=VMEM_BYTES
        ),
        cost_estimate=pl.CostEstimate(
            flops=tokens * tokens * 9 * width * 4, bytes_accessed=8 << 20,
            transcendentals=tokens * tokens * 18,
        ),
    )(
        noise_level, fine_scale, coarse_scale, image.reshape(tokens, width), cond_table, ada_fine,
        fine_qkv, fine_out_w, fine_post.reshape(1, -1), coarse_post.reshape(1, -1), merge_w,
        coarse_in_w, ada_coarse, coarse_qkv, coarse_out_w,
    )
    return fine.reshape(rows, cols, width), coarse


def solution(mesh):
    in_specs = (
        P(("noise", "row"), "col", None),
        P("noise"),
        P(),
        P(),
        P(),
        P(),
        P(),
        P(),
        P(),
        P(),
        P(),
        P(None, None, "col"),
        P("col"),
        P("col", None),
        P(),
    )
    out_specs = (P(("noise", "row"), "col", None), P(("noise", "row"), "col", None))
    return jax.shard_map(body, mesh=mesh, in_specs=in_specs, out_specs=out_specs, check_vma=False)
```

```python
import functools
import math

import jax
import jax.numpy as jnp
from jax import lax
from jax.experimental import pallas as pl
from jax.experimental.pallas import tpu as pltpu
from jax.sharding import PartitionSpec as P

HEAD = 64
TILE = 32
POOL = 8
QB = 512
VMEM_BYTES = 64 * 1024 * 1024 - 65536
EPS = 1e-6
MESH = pl.DeviceIdType.MESH
BF = jnp.bfloat16
F32 = jnp.float32
SWAP = (0, 2, 1)


def mm(a, b):
    return jnp.dot(a, b, preferred_element_type=F32)


def iota(shape, dim):
    return lax.broadcasted_iota(jnp.int32, shape, dim)


def kernel(
    nrow, ncol, level_ref, fscale_ref, cscale_ref, image_hbm, table_hbm, adaf_hbm, fqkv_hbm,
    fout_hbm, fpost_hbm, cpost_hbm, merge_hbm, cin_hbm, adac_hbm, cqkv_hbm, cout_hbm,
    fine_hbm, coarse_ref,
    slots, qs, kt, vext, acc, acc_in, table_ref, ada_fine_ref, fqkv_ref, fout_ref, fpost_ref, cpost_ref,
    merge_w, cin_w, adac_w, cqkv_w, cout_w, fine_ref, gath, pack, qall,
    sbuf, rbuf, local_sem, hsend, hrecv, gsend, grecv, rsend, rrecv, asend, arecv,
):
    tokens, width = image_hbm.shape
    image_ref = slots.at[0]
    ndev = nrow * ncol
    row, col = lax.axis_index("row"), lax.axis_index("col")
    me = row * ncol + col
    sib = 1 - 2 * lax.rem(row, 2)

    loads = [
        pltpu.make_async_copy(src, dst, local_sem.at[i])
        for i, (src, dst) in enumerate(
            ((image_hbm, image_ref), (table_hbm, table_ref), (adaf_hbm, ada_fine_ref),
             (fqkv_hbm, fqkv_ref), (adac_hbm, adac_w), (fout_hbm, fout_ref),
             (fpost_hbm, fpost_ref), (cpost_hbm, cpost_ref), (merge_hbm, merge_w),
             (cin_hbm, cin_w), (cqkv_hbm, cqkv_w), (cout_hbm, cout_w))
        )
    ]
    for load in loads:
        load.start()

    barrier = pltpu.get_barrier_semaphore()

    def greet(i, carry):
        peer = lax.rem(me + i, ndev)
        pl.semaphore_signal(
            barrier, inc=1, device_id={"row": peer // ncol, "col": lax.rem(peer, ncol)},
            device_id_type=MESH,
        )
        return carry

    lax.fori_loop(1, ndev, greet, 0)
    for load in loads[:4]:
        load.wait()
    levels = table_ref.shape[0]
    hot = iota((levels, 1), 0) == level_ref[0]
    cond = jnp.sum(jnp.where(hot, table_ref[...], 0.0), axis=0, keepdims=True)
    cond = jnp.broadcast_to(cond, (8, cond.shape[1])).T[:, 0:1]
    fine_gain = 1.0 + jnp.sum(cond * ada_fine_ref[...], axis=0, keepdims=True)
    low = iota((1, width), 1) < HEAD
    same = (iota((width, width), 0) // HEAD) == (iota((width, width), 1) // HEAD)
    block_ones = jnp.where(same, 1.0, 0.0).astype(BF)

    all_ones = jnp.ones((width, width), BF)

    def normed(x):
        x = x.astype(F32)
        total = mm((x * x).astype(BF), all_ones)
        return (x * lax.rsqrt(total * (1.0 / width) + EPS) * fine_gain).astype(BF)

    def cosine(x):
        total = mm((x * x).astype(BF), block_ones)
        return x * lax.rsqrt(total * (1.0 / HEAD) + EPS)

    factor = math.log2(math.e) / HEAD
    qscale = jnp.where(low, fscale_ref[0] * factor, fscale_ref[1] * factor)

    def make_queries(owner, slot):
        queries = cosine(mm(normed(slots[slot]), fqkv_ref[:, 0:width])) * qscale
        qs[owner, 0] = jnp.where(low, queries, 0.0).astype(BF)
        qs[owner, 1] = jnp.where(low, 0.0, queries).astype(BF)

    make_queries(0, 0)
    acc[...] = jnp.zeros_like(acc)
    loads[4].wait()
    coarse_gain = 1.0 + jnp.sum(cond * adac_w[...], axis=0, keepdims=True)

    pl.semaphore_wait(barrier, ndev - 1)

    def place(rc, bc):
        a = jnp.where(rc == 0, 0, jnp.where(rc == 1, sib, -sib))
        b = jnp.where(bc == 0, 0, jnp.where(bc == 1, -1, 1))
        r, c = row + a, col + b
        ok = (r >= 0) & (r < nrow) & (c >= 0) & (c < ncol)
        return r, c, ok

    def edge(r):
        return (r == 0) | (r == nrow - 1)

    shares = nrow > 2
    helper, helped = shares & edge(row), shares & edge(row + sib)
    blocks = tokens // QB

    def halo(rc, bc):
        r, c, ok = place(rc, bc)
        if (rc, bc) == (1, 2):
            ok = ok & jnp.logical_not(helper)
        there = SWAP[bc] * 3 + rc
        copy = pltpu.make_async_remote_copy(
            src_ref=image_ref, dst_ref=slots.at[there], send_sem=hsend.at[bc * 3 + rc],
            recv_sem=hrecv.at[there], device_id={"row": r, "col": c}, device_id_type=MESH,
        )
        return copy, ok

    order = [(1, 0), (2, 0), (0, 1), (0, 2), (1, 1), (1, 2), (2, 1), (2, 2)]
    for rc, bc in order:
        copy, ok = halo(rc, bc)

        @pl.when(ok)
        def _():
            copy.start()

    assist = pltpu.make_async_remote_copy(
        src_ref=acc.at[1], dst_ref=acc_in, send_sem=asend, recv_sem=arecv,
        device_id={"row": row + sib, "col": col}, device_id_type=MESH,
    )

    def step(s, carry):
        _, _, ok = place(lax.rem(s, 3), s // 3)
        ok = ok & jnp.logical_not(helped & (s == 4))

        @pl.when(ok)
        def _():
            @pl.when(s > 0)
            def _():
                pltpu.make_async_remote_copy(
                    src_ref=image_ref, dst_ref=slots.at[s], send_sem=hsend.at[s],
                    recv_sem=hrecv.at[s], device_id={"row": row, "col": col}, device_id_type=MESH,
                ).wait_recv()

            proj = mm(normed(slots[s]), fqkv_ref[:, width:])
            keys = cosine(proj[:, 0:width])
            kt[...] = keys.T.astype(BF)
            values = proj[:, width:]
            vext[0] = jnp.where(low, values, 1.0).astype(BF)
            vext[1] = jnp.where(low, 1.0, values).astype(BF)

            @pl.when(helper & (s == 1))
            def _():
                make_queries(1, 1)

            def blocks_of(owner):
                def block(i, c2):
                    rows = pl.ds(pl.multiple_of(i * QB, QB), QB)
                    s0 = mm(qs[owner, 0, rows, :], kt[...])
                    s1 = mm(qs[owner, 1, rows, :], kt[...])
                    p0 = jnp.exp2(s0).astype(BF)
                    acc[owner, 0, rows, :] += mm(p0, vext[0])
                    p1 = jnp.exp2(s1).astype(BF)
                    acc[owner, 1, rows, :] += mm(p1, vext[1])
                    return c2

                return block

            lax.fori_loop(jnp.where(helped & (s == 7), blocks // 2, 0), blocks, blocks_of(0), 0)
            if shares:
                extra = jnp.where(s == 3, blocks, jnp.where(s == 6, blocks // 2, 0))
                lax.fori_loop(0, jnp.where(helper, extra, 0), blocks_of(1), 0)

        if shares:
            @pl.when(helper & (s == 6))
            def _():
                assist.start()

        return carry

    lax.fori_loop(0, 9, step, 0)
    if shares:
        @pl.when(helped)
        def _():
            assist.wait_recv()
            acc[0] += acc_in[...]

    for load in loads[5:]:
        load.wait()

    a0, a1 = acc[0, 0], acc[0, 1]
    num = jnp.where(low, a0, a1)
    den = pltpu.roll(jnp.where(low, a1, a0), HEAD, 1)
    attended = (num / den).astype(BF)
    branch = mm(attended, fout_ref[...])
    branch = branch * lax.rsqrt(jnp.mean(branch * branch, axis=-1, keepdims=True) + EPS)
    fine = (slots[0].astype(F32) + branch * fpost_ref[...]).astype(BF)
    fine_ref[...] = fine
    store = pltpu.make_async_copy(fine_ref, fine_hbm, local_sem.at[len(loads)])
    store.start()
    at = iota((64, tokens), 1)
    r, c = at // TILE, at % TILE
    span = 2 * POOL
    target = ((r % 2) * 2 + c % 2) * 16 + (r // span) * (TILE // span) + c // span
    pick = jnp.where(iota((64, tokens), 0) == target, 1.0, 0.0).astype(BF)
    sums = mm(pick, fine) * (1.0 / (POOL * POOL))
    high = sums.astype(BF)
    rest = (sums - high.astype(F32)).astype(BF)
    both = jnp.concatenate(
        [
            jnp.concatenate([x[p * 16 : p * 16 + 16] for p in range(4)], axis=1)
            for x in (high, rest)
        ],
        axis=0,
    )
    pooled = mm(both, merge_w[...])
    pooled = pooled[0:16] + pooled[16:32]
    coarse_in = mm(pooled.astype(BF), cin_w[...])
    cn = coarse_in * lax.rsqrt(jnp.mean(coarse_in * coarse_in, axis=-1, keepdims=True) + EPS) * coarse_gain
    quarter = coarse_in.shape[1] // 4
    for j in range(4):
        pack[4 * j : 4 * j + 4, :] = cn[0:4, j * quarter : (j + 1) * quarter]
    gath[me] = pack[...].astype(BF)

    def gather(i):
        peer = lax.rem(me + i, ndev)
        return pltpu.make_async_remote_copy(
            src_ref=gath.at[me], dst_ref=gath.at[me], send_sem=gsend.at[i], recv_sem=grecv.at[me],
            device_id={"row": peer // ncol, "col": lax.rem(peer, ncol)}, device_id_type=MESH,
        )

    def gather_from(i):
        peer = lax.rem(me + i, ndev)
        return pltpu.make_async_remote_copy(
            src_ref=gath.at[peer], dst_ref=gath.at[peer], send_sem=gsend.at[i],
            recv_sem=grecv.at[peer],
            device_id={"row": peer // ncol, "col": lax.rem(peer, ncol)}, device_id_type=MESH,
        )

    def loop(low_at, high_at, do):
        def one(i, carry):
            do(i)
            return carry

        lax.fori_loop(low_at, high_at, one, 0)

    loop(1, ndev, lambda i: gather(i).start())
    loop(1, ndev, lambda i: gather_from(i).wait_recv())

    every = gath[...].reshape(ndev * 16, quarter)
    lw = cqkv_w.shape[2]
    count = ndev * 4
    out_at, in_at = iota((count, ndev * 16), 0), iota((count, ndev * 16), 1)
    chosen = []
    for j in range(4):
        wanted = (out_at // 4) * 16 + j * 4 + out_at % 4
        pick = jnp.where(in_at == wanted, 1.0, 0.0).astype(BF)
        chosen.append(mm(pick, every).astype(BF))
    chosen = jnp.concatenate(chosen, axis=1)
    proj = [mm(chosen, cqkv_w[k]) for k in range(3)]
    head_same = (iota((lw, lw), 0) // HEAD) == (iota((lw, lw), 1) // HEAD)
    head_ones = jnp.where(head_same, 1.0, 0.0).astype(BF)
    pair = jnp.concatenate(proj[0:2], axis=0)
    pair = pair * lax.rsqrt(mm((pair * pair).astype(BF), head_ones) * (1.0 / HEAD) + EPS)
    qall[...] = pair[0:count]
    keys = pair[count:].astype(BF)
    values = proj[2].astype(BF)
    own = ncol * 4
    queries = qall[pl.ds(pl.multiple_of(row * own, own), own), :]
    heads = lw // HEAD
    lane_head = iota((own, lw), 1) // HEAD
    stack = jnp.concatenate(
        [jnp.where(lane_head == h, queries, 0.0) for h in range(heads)], axis=0
    ).astype(BF)
    scores = lax.dot_general(stack, keys, (((1,), (1,)), ((), ())), preferred_element_type=F32)
    row_head = iota((heads * own, 1), 0) // own
    factors = jnp.zeros((heads * own, 1), F32)
    for h in range(heads):
        factors = jnp.where(row_head == h, cscale_ref[h] / HEAD, factors)
    expo = jnp.exp(scores * factors)
    weights = (expo / jnp.sum(expo, axis=-1, keepdims=True)).astype(BF)
    mixed = jnp.where(iota((heads * own, lw), 1) // HEAD == row_head, mm(weights, values), 0.0)
    results = sum(mixed[h * own : (h + 1) * own] for h in range(heads))
    partial = mm(results.astype(BF), cout_w[...])
    for k in range(ncol):
        for j in range(4):
            pack[4 * j : 4 * j + 4, :] = partial[4 * k : 4 * k + 4, j * quarter : (j + 1) * quarter]
        sbuf[k] = pack[...].astype(BF)
    rbuf[col] = sbuf[col]

    def reduce(i):
        peer = lax.rem(col + i, ncol)
        return pltpu.make_async_remote_copy(
            src_ref=sbuf.at[peer], dst_ref=rbuf.at[col], send_sem=rsend.at[i],
            recv_sem=rrecv.at[col], device_id={"row": row, "col": peer}, device_id_type=MESH,
        )

    def reduce_from(i):
        peer = lax.rem(col + i, ncol)
        return pltpu.make_async_remote_copy(
            src_ref=sbuf.at[peer], dst_ref=rbuf.at[peer], send_sem=rsend.at[i],
            recv_sem=rrecv.at[peer], device_id={"row": row, "col": peer}, device_id_type=MESH,
        )

    loop(1, ncol, lambda i: reduce(i).start())
    loop(1, ncol, lambda i: reduce_from(i).wait_recv())
    total = jnp.sum(rbuf[...].astype(F32), axis=0)
    pack[...] = total
    pieces = [pack[4 * j : 4 * j + 4, :] for j in range(4)]
    power = sum(jnp.sum(piece * piece, axis=-1, keepdims=True) for piece in pieces)
    inverse = lax.rsqrt(power * (1.0 / (4 * quarter)) + EPS)
    for j in range(4):
        at_j = slice(j * quarter, (j + 1) * quarter)
        y = coarse_in[0:4, at_j] + pieces[j] * inverse * cpost_ref[:, at_j]
        for k in range(coarse_ref.shape[0]):
            side = coarse_ref.shape[1]
            coarse_ref[k, :, at_j] = y[k * side : (k + 1) * side].astype(BF)

    store.wait()

    if shares:
        @pl.when(helper)
        def _():
            assist.wait_send()

    for rc, bc in order:
        copy, ok = halo(rc, bc)

        @pl.when(ok)
        def _():
            copy.wait_send()

    loop(1, ndev, lambda i: gather(i).wait_send())
    loop(1, ncol, lambda i: reduce(i).wait_send())


def writer(fine_ref, coarse_ref, fine_out_ref, coarse_out_ref):
    fine_out_ref[...] = fine_ref[...]
    coarse_out_ref[...] = coarse_ref[...]


def body(
    image, noise_level, cond_table, ada_fine, fine_qkv, fine_scale, fine_out_w, fine_post,
    merge_w, coarse_in_w, ada_coarse, coarse_qkv, coarse_scale, coarse_out_w, coarse_post,
):
    nrow, ncol = lax.axis_size("row"), lax.axis_size("col")
    ndev = nrow * ncol
    rows, cols, width = image.shape
    tokens = rows * cols
    lw = coarse_qkv.shape[2]
    cw = coarse_in_w.shape[1]
    quarter = cw // 4
    side = TILE // (2 * POOL)
    smem = pl.BlockSpec(memory_space=pltpu.SMEM)
    vmem = pl.BlockSpec(memory_space=pltpu.VMEM)
    hbm = pl.BlockSpec(memory_space=pl.ANY)
    dma = pltpu.SemaphoreType.DMA
    fine, coarse = pl.pallas_call(
        functools.partial(kernel, nrow, ncol),
        out_shape=(
            jax.ShapeDtypeStruct((tokens, width), BF),
            jax.ShapeDtypeStruct((side, side, cw), BF),
        ),
        in_specs=[smem] * 3 + [hbm] * 12,
        out_specs=(hbm, vmem),
        scratch_shapes=[
            pltpu.VMEM((9, tokens, width), BF),
            pltpu.VMEM((2, 2, tokens, width), BF),
            pltpu.VMEM((width, tokens), BF),
            pltpu.VMEM((2, tokens, width), BF),
            pltpu.VMEM((2, 2, tokens, width), F32),
            pltpu.VMEM((2, tokens, width), F32),
            pltpu.VMEM(cond_table.shape, F32),
            pltpu.VMEM(ada_fine.shape, F32),
            pltpu.VMEM(fine_qkv.shape, BF),
            pltpu.VMEM(fine_out_w.shape, BF),
            pltpu.VMEM((1, width), F32),
            pltpu.VMEM((1, cw), F32),
            pltpu.VMEM(merge_w.shape, BF),
            pltpu.VMEM(coarse_in_w.shape, BF),
            pltpu.VMEM(ada_coarse.shape, F32),
            pltpu.VMEM(coarse_qkv.shape, BF),
            pltpu.VMEM(coarse_out_w.shape, BF),
            pltpu.VMEM((tokens, width), BF),
            pltpu.VMEM((ndev, 16, quarter), BF),
            pltpu.VMEM((16, quarter), F32),
            pltpu.VMEM((ndev * 4, lw), F32),
            pltpu.VMEM((ncol, 16, quarter), BF),
            pltpu.VMEM((ncol, 16, quarter), BF),
            dma((13,)), dma((9,)), dma((9,)), dma((ndev,)), dma((ndev,)), dma((ncol,)), dma((ncol,)),
            dma, dma,
        ],
        compiler_params=pltpu.CompilerParams(
            collective_id=0, has_side_effects=True, vmem_limit_bytes=VMEM_BYTES
        ),
        cost_estimate=pl.CostEstimate(
            flops=tokens * tokens * 9 * width * 4, bytes_accessed=8 << 20,
            transcendentals=tokens * tokens * 18,
        ),
    )(
        noise_level, fine_scale, coarse_scale, image.reshape(tokens, width), cond_table, ada_fine,
        fine_qkv, fine_out_w, fine_post.reshape(1, -1), coarse_post.reshape(1, -1), merge_w,
        coarse_in_w, ada_coarse, coarse_qkv, coarse_out_w,
    )
    fine, coarse = pl.pallas_call(
        writer,
        out_shape=(
            jax.ShapeDtypeStruct(fine.shape, BF),
            jax.ShapeDtypeStruct(coarse.shape, BF),
        ),
        in_specs=[vmem, vmem],
        out_specs=(vmem, vmem),
        compiler_params=pltpu.CompilerParams(vmem_limit_bytes=VMEM_BYTES),
    )(fine, coarse)
    return fine.reshape(rows, cols, width), coarse


def solution(mesh):
    in_specs = (
        P(("noise", "row"), "col", None),
        P("noise"),
        P(),
        P(),
        P(),
        P(),
        P(),
        P(),
        P(),
        P(),
        P(),
        P(None, None, "col"),
        P("col"),
        P("col", None),
        P(),
    )
    out_specs = (P(("noise", "row"), "col", None), P(("noise", "row"), "col", None))
    return jax.shard_map(body, mesh=mesh, in_specs=in_specs, out_specs=out_specs, check_vma=False)
```
